128 devices in a mesh: rep: 8 (over y, x_lo), fsdp: 16 (over z, x_hi, core).
Axes of the slice: x: 4 (x_hi: 2, x_lo: 2; x = x_hi * 2 + x_lo), y: 4, z: 4, core: 2. Of those that a mesh axis runs over, the one named last changes fastest.
Arguments:
- tokens: bfloat16 [16384, 1152], P(('rep', 'fsdp')), may hold values from -6 to 6
- lengths: int32 [8, 4], P('rep'), may hold values from 1 to 1536, 2048 in all within a row
- cotangent: bfloat16 [16384, 1152], P(('rep', 'fsdp')), may hold values from -6 to 6
- pre_attention: bfloat16 [1152], P('fsdp'), may hold values from 0.5 to 1.5
- post_attention: bfloat16 [1152], P('fsdp'), may hold values from 0.5 to 1.5
- pre_forward: bfloat16 [1152], P('fsdp'), may hold values from 0.5 to 1.5
- post_forward: bfloat16 [1152], P('fsdp'), may hold values from 0.5 to 1.5
- query_gain: bfloat16 [256], P('fsdp'), may hold values from 0.5 to 1.5
- key_gain: bfloat16 [256], P('fsdp'), may hold values from 0.5 to 1.5
- query_weight: bfloat16 [1152, 1024], P('fsdp'), may hold values from -0.1875 to 0.1875
- key_weight: bfloat16 [1152, 256], P('fsdp'), may hold values from -0.1875 to 0.1875
- value_weight: bfloat16 [1152, 256], P('fsdp'), may hold values from -0.1875 to 0.1875
- output_weight: bfloat16 [1024, 1152], P('fsdp'), may hold values from -0.1875 to 0.1875
- gate_rows: bfloat16 [6912, 1152], P('fsdp'), may hold values from -0.1875 to 0.1875
- up_rows: bfloat16 [6912, 1152], P('fsdp'), may hold values from -0.1875 to 0.1875
- down_rows: bfloat16 [6912, 1152], P('fsdp'), may hold values from -0.078125 to 0.078125
Outputs:
- output: bfloat16 [16384, 1152], P(('rep', 'fsdp'))
- grad_tokens: float32 [16384, 1152], P(('rep', 'fsdp'))
- grad_pre_attention: float32 [1152], P('fsdp')
- grad_post_attention: float32 [1152], P('fsdp')
- grad_pre_forward: float32 [1152], P('fsdp')
- grad_post_forward: float32 [1152], P('fsdp')
- grad_query_gain: float32 [256], P('fsdp')
- grad_key_gain: float32 [256], P('fsdp')
- grad_query_weight: float32 [1152, 1024], P('fsdp')
- grad_key_weight: float32 [1152, 256], P('fsdp')
- grad_value_weight: float32 [1152, 256], P('fsdp')
- grad_output_weight: float32 [1024, 1152], P('fsdp')
- grad_gate_rows: float32 [6912, 1152], P('fsdp')
- grad_up_rows: float32 [6912, 1152], P('fsdp')
- grad_down_rows: float32 [6912, 1152], P('fsdp')
The draws below stay inside these ranges and needn't reach their ends.
Inputs may be any that keep to these rules, and one draw needn't show every extreme that they name: Each row lists the lengths of 4 documents that fill one replica group's 2048 tokens in order; a row sums to 2048 and its longest document has exactly 1536 tokens.
All inputs are finite; a program needn't handle non-finite values.
Results may differ from the reference program's by a relative error of at most 0.028.
Values may be sent and summed in bfloat16 or wider, within the bound.
No kernel may reach another device: no remote copies, remote signals or barrier semaphores. Data moves between devices by JAX's collectives and lax.ppermute only.
A program may use at most 128 MiB of HBM per device.

```python
import math
import jax
import jax.numpy as jnp
import numpy as np
from jax import lax

D = 1152
H = 4
HD = 256
FF = 6912
WINDOW = 512
NDOC = 4
HQ = 1024
GROUP = 2048
MAX_LEN = 1536
TOKENS = 16384
N_REP = 8


def steps_of(rng, extent, pieces, least, top_value):
    level, own = 1.0, jax.random.fold_in(rng, 6)
    for dim, blocks in pieces:
        draws = jnp.exp(jax.random.uniform(jax.random.fold_in(own, dim), (blocks,), jnp.float32, least / len(pieces), top_value / len(pieces)))
        level = level * jnp.repeat(draws, extent[dim] // blocks).reshape([-1 if axis == dim else 1 for axis in range(len(extent))])
    return level


def length_profile(count, total, reach, lean):
    loads = [(1 << 20) // math.isqrt(grade ** lean) + 1 for grade in range(2, count + 1)]
    rest, counts = total - reach - (count - 1), [1] * (count - 1)
    while rest > 0:
        free = [i for i in range(count - 1) if counts[i] < reach]
        whole, left = sum([loads[i] for i in free]), rest
        for i in free:
            extra = min(reach - counts[i], max(1, left * loads[i] // whole), rest)
            counts[i] = counts[i] + extra
            rest = rest - extra
    return np.array([reach] + counts)


def ragged_sizes(key, count, total, limit, slope):
    if count == 2:
        one = jax.random.randint(key, (), max(1, total - limit), min(limit, total - 1) + 1)
        return jnp.stack([one, total - one])
    sizes = jnp.asarray(length_profile(count, total, limit, slope), jnp.int32)
    pairs = (count - 1) // 2
    donor, receiver = sizes[1:1 + 2 * pairs:2], sizes[2:2 + 2 * pairs:2]
    room = jnp.minimum(donor - 1, limit - receiver)
    shifted = jax.random.randint(jax.random.fold_in(key, 1), (pairs,), 0, 1 << 20) % (room + 1)
    sizes = sizes.at[1:1 + 2 * pairs:2].set(donor - shifted).at[2:2 + 2 * pairs:2].set(receiver + shifted)
    return sizes[jax.random.permutation(jax.random.fold_in(key, 2), count)]


def gaussian(own_key, extent, spread, most, shards=(), kind=jnp.bfloat16):
    drawn = spread * jax.random.normal(own_key, extent, jnp.float32)
    if shards:
        drawn = drawn * steps_of(own_key, extent, shards, -0.22, 0.18)
    return jnp.clip(drawn, -most, most).astype(kind)


def setup_inputs(seed: int = 0) -> dict:
    key_of = jax.random.split(jax.random.key(seed), 17)
    return {
        "tokens": gaussian(key_of[0], (TOKENS, D), 1.0, 6.0, ((0, 128),)),
        "lengths": jax.vmap(lambda own: ragged_sizes(own, NDOC, GROUP, MAX_LEN, 2))(jax.random.split(key_of[1], N_REP)).reshape((N_REP, NDOC)).astype(jnp.int32),
        "cotangent": gaussian(key_of[2], (TOKENS, D), 1.0, 6.0, ((0, 128),)),
        "pre_attention": jnp.clip(1.0 + 0.1 * jax.random.normal(key_of[3], (D,), jnp.float32), 0.5, 1.5).astype(jnp.bfloat16),
        "post_attention": jnp.clip(1.0 + 0.1 * jax.random.normal(key_of[4], (D,), jnp.float32), 0.5, 1.5).astype(jnp.bfloat16),
        "pre_forward": jnp.clip(1.0 + 0.1 * jax.random.normal(key_of[5], (D,), jnp.float32), 0.5, 1.5).astype(jnp.bfloat16),
        "post_forward": jnp.clip(1.0 + 0.1 * jax.random.normal(key_of[6], (D,), jnp.float32), 0.5, 1.5).astype(jnp.bfloat16),
        "query_gain": jnp.clip(1.0 + 0.1 * jax.random.normal(key_of[7], (HD,), jnp.float32), 0.5, 1.5).astype(jnp.bfloat16),
        "key_gain": jnp.clip(1.0 + 0.1 * jax.random.normal(key_of[8], (HD,), jnp.float32), 0.5, 1.5).astype(jnp.bfloat16),
        "query_weight": gaussian(key_of[9], (D, HQ), D ** -0.5, 0.1875, ((0, 16),)),
        "key_weight": gaussian(key_of[10], (D, HD), D ** -0.5, 0.1875, ((0, 16),)),
        "value_weight": gaussian(key_of[11], (D, HD), D ** -0.5, 0.1875, ((0, 16),)),
        "output_weight": gaussian(key_of[12], (HQ, D), HQ ** -0.5, 0.1875, ((0, 16),)),
        "gate_rows": gaussian(key_of[13], (FF, D), D ** -0.5, 0.1875, ((0, 16),)),
        "up_rows": gaussian(key_of[14], (FF, D), D ** -0.5, 0.1875, ((0, 16),)),
        "down_rows": gaussian(key_of[15], (FF, D), FF ** -0.5, 0.078125, ((0, 16),)),
    }


@jax.custom_vjp
def low(v):
    return lax.optimization_barrier(v.astype(jnp.bfloat16)).astype(jnp.float32)

@jax.custom_vjp
def low_back(v):
    return v

def low_keep(v):
    return (low(v), None)

def low_pass(kept, grad):
    return (grad,)

def back_keep(v):
    return (v, None)

def back_low(kept, grad):
    return (low(grad),)
low.defvjp(low_keep, low_pass)
low_back.defvjp(back_keep, back_low)
HIGH = lax.Precision.HIGHEST
EPSILON = 1e-06
MASKED = -1e+30

def norm_rows(values, gain):
    return values * lax.rsqrt(lax.optimization_barrier(jnp.mean(values * values, axis=-1, keepdims=True)) + EPSILON) * gain

def rotate(values, position):
    half = values.shape[-1] // 2
    freq = 10000.0 ** (-2.0 * jnp.arange(half, dtype=jnp.float32) / values.shape[-1])
    angle = position.astype(jnp.float32)[:, None] * freq[None, :]
    cosine = jnp.cos(angle)[:, None, :]
    sine = jnp.sin(angle)[:, None, :]
    first = values[..., :half]
    second = values[..., half:]
    return jnp.concatenate([first * cosine - second * sine, second * cosine + first * sine], axis=-1)

def doc_info(lengths, index):
    ends = jnp.cumsum(lengths)
    starts = ends - lengths
    segment = lax.optimization_barrier(jnp.sum((index[:, None] >= ends[None, :-1]).astype(jnp.int32), axis=1))
    hit = segment[:, None] == jnp.arange(lengths.shape[0], dtype=jnp.int32)[None, :]
    first = lax.optimization_barrier(jnp.sum(jnp.where(hit, starts[None, :], 0), axis=1)).astype(jnp.int32)
    segment = jnp.where(index < 0, -1, segment).astype(jnp.int32)
    return (segment, (index - first).astype(jnp.int32))

def attention(queries, keys, values, segment, index):
    block_rows = min(512, GROUP)
    padded_keys = jnp.pad(keys, ((WINDOW, 0), (0, 0)))
    padded_values = jnp.pad(values, ((WINDOW, 0), (0, 0)))
    padded_segment = jnp.concatenate([jnp.full((WINDOW,), -1, jnp.int32), segment])
    padded_index = jnp.concatenate([jnp.arange(-WINDOW, 0, dtype=jnp.int32), index])

    def one_block(number):
        start = (number * block_rows).astype(jnp.int32)
        query_block = lax.dynamic_slice_in_dim(queries, start, block_rows, 0)
        key_block = lax.dynamic_slice_in_dim(padded_keys, start, block_rows + WINDOW, 0)
        value_block = lax.dynamic_slice_in_dim(padded_values, start, block_rows + WINDOW, 0)
        query_seg = lax.dynamic_slice_in_dim(segment, start, block_rows, 0)
        query_idx = lax.dynamic_slice_in_dim(index, start, block_rows, 0)
        key_seg = lax.dynamic_slice_in_dim(padded_segment, start, block_rows + WINDOW, 0)
        key_idx = lax.dynamic_slice_in_dim(padded_index, start, block_rows + WINDOW, 0)
        distance = query_idx[:, None] - key_idx[None, :]
        allowed = (query_seg[:, None] == key_seg[None, :]) & (distance >= 0) & (distance < WINDOW)
        scores = low_back(jnp.einsum('thd,kd->htk', query_block, key_block, precision=HIGH))
        scores = jnp.where(allowed[None], scores, MASKED)
        expo = jnp.exp(scores - lax.optimization_barrier(jnp.max(scores, axis=-1, keepdims=True)))
        probs = low(expo / lax.optimization_barrier(jnp.sum(expo, axis=-1, keepdims=True)))
        return jnp.einsum('htk,kd->thd', probs, value_block, precision=HIGH)
    mixed = lax.map(jax.checkpoint(one_block), jnp.arange(GROUP // block_rows, dtype=jnp.int32))
    return mixed.reshape(GROUP, H * HD)

def layer(inputs, weights, segment, position, index):
    pre_attention, post_attention, pre_forward, post_forward, query_gain, key_gain, query_weight, key_weight, value_weight, output_weight, gate_rows, up_rows, down_rows = weights
    normed_one = low(norm_rows(inputs, pre_attention))
    query_lin = low_back(jnp.dot(normed_one, query_weight, precision=HIGH)).reshape(GROUP, H, HD)
    key_lin = low_back(jnp.dot(normed_one, key_weight, precision=HIGH))
    values = low(low_back(jnp.dot(normed_one, value_weight, precision=HIGH)))
    queries = low_back(low(rotate(norm_rows(query_lin, query_gain), position) * HD ** (-0.5)))
    keys = low_back(low(rotate(norm_rows(key_lin[:, None, :], key_gain), position)[:, 0, :]))
    mixed = low_back(low(attention(queries, keys, values, segment, index)))
    projected = low_back(jnp.dot(mixed, output_weight, precision=HIGH))
    residual_one = inputs + norm_rows(projected, post_attention)
    normed_two = low(norm_rows(residual_one, pre_forward))
    gate = low_back(jnp.dot(normed_two, gate_rows.T, precision=HIGH))
    upward = low_back(jnp.dot(normed_two, up_rows.T, precision=HIGH))
    hidden = low(jax.nn.gelu(gate, approximate=True) * upward)
    down_sum = low_back(jnp.dot(hidden, down_rows, precision=HIGH))
    return residual_one + norm_rows(down_sum, post_forward)

def reference(tokens, lengths, cotangent, pre_attention, post_attention, pre_forward, post_forward, query_gain, key_gain, query_weight, key_weight, value_weight, output_weight, gate_rows, up_rows, down_rows):
    weights = tuple((item.astype(jnp.float32) for item in (pre_attention, post_attention, pre_forward, post_forward, query_gain, key_gain, query_weight, key_weight, value_weight, output_weight, gate_rows, up_rows, down_rows)))
    inputs = tokens.astype(jnp.float32).reshape(N_REP, GROUP, D)
    grads_in = cotangent.astype(jnp.float32).reshape(N_REP, GROUP, D)
    index = jnp.arange(GROUP, dtype=jnp.int32)

    def one_group(totals, item):
        group_in, group_grad, group_lengths = item
        segment, position = doc_info(group_lengths, index)

        def apply_layer(values, params):
            return layer(values, params, segment, position, index)
        result, pull = jax.vjp(apply_layer, group_in, weights)
        grad_values, grad_params = pull(group_grad)
        totals = jax.tree.map(jnp.add, totals, grad_params)
        return (totals, (result.astype(jnp.bfloat16), grad_values))
    zeros = jax.tree.map(jnp.zeros_like, weights)
    grads, (results, grad_inputs) = lax.scan(one_group, zeros, (inputs, grads_in, lengths))
    return (results.reshape(TOKENS, D), grad_inputs.reshape(TOKENS, D), grads[0], grads[1], grads[2], grads[3], grads[4], grads[5], grads[6], grads[7], grads[8], grads[9], grads[10], grads[11], grads[12])
```

```python
import jax
import jax.numpy as jnp
from jax import lax
from jax.sharding import PartitionSpec as P

WINDOW = 512
EPSILON = 1e-06
MASKED = -1e30
CONTRACT_LAST = (((1,), (1,)), ((), ()))
CONTRACT_FIRST = (((0,), (0,)), ((), ()))
F32 = jnp.float32
LOW = jnp.bfloat16
NZ, NH, NC = (4, 2, 2)
PEERS = [(1, 0), (3, 0), (0, 1), (1, 1), (3, 1), (2, 0), (2, 1)]
CHIPS = [(0, 0)] + PEERS
PAIRS = [((0, 0), (0, 1)), ((1, 0), (3, 0)), ((1, 1), (3, 1)), ((2, 0), (2, 1))]


def place(z, h, c):
    return (z % NZ * NH + h % NH) * NC + c % NC


def route(dz, dh, dc):
    return [
        (place(z + dz, h + dh, c + dc), place(z, h, c))
        for z in range(NZ)
        for h in range(NH)
        for c in range(NC)
    ]


def fetch(block, dz, dh, dc=0):
    return lax.ppermute(block, "fsdp", route(dz, dh, dc))


def hand(block, dz, dh, dc=0):
    return fetch(block, -dz, -dh, -dc)


def swap(block):
    return fetch(block, 0, 0, 1)


def gather_chips(block):
    blocks = {(0, 0): block}
    for peer in PEERS:
        blocks[peer] = fetch(block, *peer)
    return blocks


def coordinates():
    me = lax.axis_index("fsdp")
    return (me // (NH * NC), me // NC % NH, me % NC)


def turned(blocks, start):
    twice = jnp.concatenate([blocks, blocks], axis=0)
    return lax.dynamic_slice_in_dim(twice, start, NZ, 0)


def flipped(blocks, amount, axis):
    return jnp.where(amount == 0, blocks, jnp.flip(blocks, axis))


def to_relative(lines):
    z, h, c = coordinates()
    blocks = lines.reshape(NZ, NH, NC, -1, *lines.shape[1:])
    return flipped(flipped(turned(blocks, z), h, 1), c, 2).reshape(lines.shape)


def to_mesh_order(lines):
    z, h, c = coordinates()
    blocks = lines.reshape(NZ, NH, NC, -1, *lines.shape[1:])
    return flipped(flipped(turned(blocks, (NZ - z) % NZ), h, 1), c, 2).reshape(lines.shape)


def in_offset_order(chips):
    mine = jnp.stack([chips[z, h] for z in range(NZ) for h in range(NH)])
    other = swap(mine)
    both = jnp.stack([mine, other], axis=1)
    return both.reshape(NZ * NH * NC, *mine.shape[1:])


def scatter_sum(blocks):
    chips = blocks.reshape(NZ, NH, NC, *blocks.shape[1:])
    away = swap(chips[:, :, 1].astype(LOW))
    both = chips[:, :, 0].astype(F32) + away.astype(F32)
    total = both[0, 0]
    low = both.astype(LOW)
    for z, h in PEERS:
        total = total + hand(low[z, h], z, h).astype(F32)
    return total


def rep_sum(x):
    copies = jnp.broadcast_to(x.astype(LOW), (lax.axis_size("rep"), *x.shape))
    everything = lax.all_to_all(copies, "rep", split_axis=0, concat_axis=0, tiled=True)
    return jnp.sum(everything.astype(F32), axis=0)


def rep_sum_by_parts(x):
    parts = lax.axis_size("rep")
    lines = x.astype(LOW).reshape(parts, -1, x.shape[1])
    arrived = lax.all_to_all(lines, "rep", split_axis=0, concat_axis=0, tiled=True)
    own = jnp.sum(arrived.astype(F32), axis=0).astype(LOW)
    copies = jnp.broadcast_to(own, (parts, *own.shape))
    whole = lax.all_to_all(copies, "rep", split_axis=0, concat_axis=0, tiled=True)
    return whole.reshape(x.shape).astype(F32)


def shifted(block, axis, distance):
    devices = range(lax.axis_size(axis))
    pairs = [(i - distance, i) for i in devices if i - distance in devices]
    return lax.ppermute(block, axis, pairs)


def norm_rows(values, gain):
    return values * lax.rsqrt(jnp.mean(values * values, axis=-1, keepdims=True) + EPSILON) * gain


def rotate(values, position):
    half = values.shape[-1] // 2
    freq = 10000.0 ** (-2.0 * jnp.arange(half, dtype=F32) / values.shape[-1])
    angle = position.astype(F32)[:, None] * freq[None, :]
    cosine = jnp.cos(angle)[:, None, :]
    sine = jnp.sin(angle)[:, None, :]
    first = values[..., :half]
    second = values[..., half:]
    return jnp.concatenate(
        [first * cosine - second * sine, second * cosine + first * sine], axis=-1
    )


def doc_info(lengths, index):
    ends = jnp.cumsum(lengths)
    starts = ends - lengths
    segment = jnp.sum((index[:, None] >= ends[None, :-1]).astype(jnp.int32), axis=1)
    hit = segment[:, None] == jnp.arange(lengths.shape[0], dtype=jnp.int32)[None, :]
    first = jnp.sum(jnp.where(hit, starts[None, :], 0), axis=1)
    segment = jnp.where(index < 0, -1, segment)
    return (segment, index - first)


def activate(gate, upward):
    return jax.nn.gelu(gate, approximate=True) * upward


def dot(a, b, dims=(((1,), (0,)), ((), ()))):
    return lax.dot_general(a, b, dims, preferred_element_type=F32)


def local(
    tokens,
    lengths,
    cotangent,
    pre_attention,
    post_attention,
    pre_forward,
    post_forward,
    query_gain,
    key_gain,
    query_weight,
    key_weight,
    value_weight,
    output_weight,
    gate_rows,
    up_rows,
    down_rows,
):
    rows = tokens.shape[0]
    width = tokens.shape[1]
    head_size = key_weight.shape[1]
    heads = query_weight.shape[1] // head_size
    features = heads * head_size
    span = features + 2 * head_size
    devices = NZ * NH * NC
    own_rows = query_weight.shape[0]
    own_gain = query_gain.shape[0]
    blocks_back = (WINDOW + rows - 1) // rows
    shard = lax.axis_index("fsdp")
    local_index = shard * rows + jnp.arange(rows, dtype=jnp.int32)
    key_index = (shard - blocks_back) * rows + jnp.arange(rows * (blocks_back + 1), dtype=jnp.int32)
    query_seg, query_pos = doc_info(lengths[0], local_index)
    key_seg, key_place = doc_info(lengths[0], key_index)
    distance = local_index[:, None] - key_index[None, :]
    allowed = (query_seg[:, None] == key_seg[None, :]) & (distance >= 0) & (distance < WINDOW)

    gains = jnp.concatenate(
        [pre_attention, post_attention, pre_forward, post_forward, query_gain, key_gain]
    )
    gain_line = jnp.pad(gains[None, :], ((0, 7), (0, span - gains.shape[0])))
    packed = jnp.concatenate(
        [jnp.concatenate([query_weight, key_weight, value_weight], axis=1), gain_line], axis=0
    )
    first_all = in_offset_order(gather_chips(packed))
    weight_in = first_all[:, :own_rows].reshape(width, span)
    weight_out = in_offset_order(gather_chips(output_weight)).reshape(features, width)
    gain_all = to_mesh_order(first_all[:, own_rows, : gains.shape[0]]).astype(F32)
    gain_pre_att, gain_post_att, gain_pre_fwd, gain_post_fwd = (
        gain_all[:, k * own_rows : (k + 1) * own_rows].reshape(width) for k in range(4)
    )
    gain_query, gain_key = (
        gain_all[:, 4 * own_rows + k * own_gain : 4 * own_rows + (k + 1) * own_gain].reshape(
            head_size
        )
        for k in range(2)
    )
    gate_both = jnp.concatenate([gate_rows, swap(gate_rows)], axis=0)
    up_both = jnp.concatenate([up_rows, swap(up_rows)], axis=0)
    down_both = jnp.concatenate([down_rows, swap(down_rows)], axis=0)

    inputs = tokens.astype(F32)
    normed_one, pull_one = jax.vjp(norm_rows, inputs, gain_pre_att)
    normed_low = normed_one.astype(LOW)
    normed_rel = to_relative(normed_low.T.reshape(devices, own_rows, rows)).reshape(width, rows)
    linear = dot(normed_rel, weight_in, CONTRACT_FIRST)
    query_lin = linear[:, :features]
    key_lin = linear[:, features : features + head_size]
    value_low = linear[:, features + head_size :].astype(LOW)

    def query_side(lin, gain):
        return rotate(
            norm_rows(lin.reshape(rows, heads, head_size), gain), query_pos
        ) * head_size ** (-0.5)

    def key_side(lin, gain):
        return rotate(norm_rows(lin[:, None, :], gain), query_pos)[:, 0, :]

    query_value, pull_query = jax.vjp(query_side, query_lin, gain_query)
    key_value, pull_key = jax.vjp(key_side, key_lin, gain_key)
    query_low = query_value.astype(LOW)
    key_low = key_value.astype(LOW)
    outgoing = jnp.concatenate([key_low, value_low], axis=1)
    arrived = []
    for step in range(blocks_back, 0, -1):
        arrived.append(shifted(outgoing, "fsdp", step))
    both = jnp.concatenate(arrived + [outgoing], axis=0)
    keys_all = both[:, :head_size]
    values_all = both[:, head_size:]
    scores = jnp.einsum("thd,kd->htk", query_low, keys_all, preferred_element_type=F32)
    scores = jnp.where(allowed[None], scores, MASKED)
    peak = jnp.max(scores, axis=-1, keepdims=True)
    expo = jnp.exp(scores - peak)
    total = jnp.sum(expo, axis=-1, keepdims=True)
    probs = expo / total
    probs_low = probs.astype(LOW)
    mixed = jnp.einsum("htk,kd->thd", probs_low, values_all, preferred_element_type=F32)
    mixed_low = mixed.reshape(rows, features).astype(LOW)
    mixed_rel = to_relative(mixed_low.T.reshape(devices, -1, rows)).reshape(features, rows)
    projected = dot(mixed_rel, weight_out, CONTRACT_FIRST)
    attended, pull_two = jax.vjp(norm_rows, projected, gain_post_att)
    residual_one = inputs + attended
    normed_two, pull_three = jax.vjp(norm_rows, residual_one, gain_pre_fwd)
    normed_two_low = normed_two.astype(LOW)

    normed_of = gather_chips(normed_two_low)
    acts = []
    partial = {}
    for pair in PAIRS:
        block = jnp.concatenate([normed_of[p] for p in pair], axis=0)
        gate = dot(block, gate_both, CONTRACT_LAST)
        upward = dot(block, up_both, CONTRACT_LAST)
        hidden = activate(gate, upward).astype(LOW)
        down = dot(hidden, down_both)
        acts.append((block, gate, upward, hidden))
        for k, p in enumerate(pair):
            partial[p] = down[k * rows : (k + 1) * rows]
    down_sum = partial[0, 0]
    for p in PEERS:
        down_sum = down_sum + hand(partial[p].astype(LOW), *p).astype(F32)
    fed, pull_four = jax.vjp(norm_rows, down_sum, gain_post_fwd)
    output = (residual_one + fed).astype(LOW)
    grad_out = cotangent.astype(F32)
    grad_down, grad_post_fwd = pull_four(grad_out)
    grad_down_of = gather_chips(grad_down.astype(LOW))
    saved = []
    partial = {}
    for pair, (block, gate, upward, hidden) in zip(PAIRS, acts):
        grad_block = jnp.concatenate([grad_down_of[p] for p in pair], axis=0)
        grad_hidden = dot(grad_block, down_both, CONTRACT_LAST)
        _, pull = jax.vjp(activate, gate, upward)
        grad_gate, grad_up = pull(grad_hidden)
        gate_low, up_low = (grad_gate.astype(LOW), grad_up.astype(LOW))
        back = dot(gate_low, gate_both) + dot(up_low, up_both)
        saved.append((block, grad_block, gate_low, up_low, hidden))
        for k, p in enumerate(pair):
            partial[p] = back[k * rows : (k + 1) * rows]
    grad_normed_two = partial[0, 0]
    for p in PEERS:
        grad_normed_two = grad_normed_two + hand(partial[p].astype(LOW), *p).astype(F32)
    whole = [jnp.concatenate(parts, axis=0) for parts in zip(*saved)]
    group_normed, group_grad, group_gate, group_up, group_hidden = whole
    row_grads = jnp.concatenate(
        [
            dot(group_gate, group_normed, CONTRACT_FIRST),
            dot(group_up, group_normed, CONTRACT_FIRST),
            dot(group_hidden, group_grad, CONTRACT_FIRST),
        ],
        axis=1,
    )
    hidden_rows = gate_rows.shape[0]
    owned_rows = row_grads[:hidden_rows] + swap(row_grads[hidden_rows:].astype(LOW)).astype(F32)
    spare = -hidden_rows % 64
    owned_rows = rep_sum_by_parts(jnp.pad(owned_rows.astype(LOW), ((0, spare), (0, 0))))
    owned_rows = owned_rows[:hidden_rows]

    extra_three, grad_pre_fwd = pull_three(grad_normed_two)
    grad_residual = grad_out + extra_three
    grad_projected, grad_post_att = pull_two(grad_residual)
    grad_proj_low = grad_projected.astype(LOW)
    grad_mixed_rel = dot(weight_out, grad_proj_low, CONTRACT_LAST).astype(LOW)
    grad_mixed_low = to_mesh_order(grad_mixed_rel.reshape(devices, -1, rows))
    grad_mixed_low = grad_mixed_low.reshape(features, rows).T
    grad_output_weight = dot(mixed_rel, grad_proj_low).reshape(devices, -1, width)
    owned_output = rep_sum(scatter_sum(grad_output_weight))
    grad_mixed_heads = grad_mixed_low.reshape(rows, heads, head_size)
    grad_probs = jnp.einsum("thd,kd->htk", grad_mixed_heads, values_all, preferred_element_type=F32)
    inner = jnp.sum(grad_probs * probs, axis=-1, keepdims=True)
    grad_scores = (probs * (grad_probs - inner)).astype(LOW)
    grad_query_low = jnp.einsum(
        "htk,kd->thd", grad_scores, keys_all, preferred_element_type=F32
    ).astype(LOW)
    grad_keys_all = jnp.einsum("htk,thd->kd", grad_scores, query_low, preferred_element_type=F32)
    grad_values_all = jnp.einsum(
        "htk,thd->kd", probs_low, grad_mixed_heads, preferred_element_type=F32
    )
    grad_both = jnp.concatenate([grad_keys_all, grad_values_all], axis=1)
    owned_both = grad_both[blocks_back * rows :]
    for step in range(1, blocks_back + 1):
        piece = grad_both[(blocks_back - step) * rows : (blocks_back - step + 1) * rows]
        owned_both = owned_both + shifted(piece.astype(LOW), "fsdp", -step).astype(F32)
    grad_key_low = owned_both[:, :head_size].astype(LOW)
    grad_value_low = owned_both[:, head_size:].astype(LOW)
    grad_query_lin, grad_query_gain = pull_query(grad_query_low.astype(F32))
    grad_key_lin, grad_key_gain = pull_key(grad_key_low.astype(F32))
    grad_linear = jnp.concatenate(
        [grad_query_lin.astype(LOW), grad_key_lin.astype(LOW), grad_value_low], axis=1
    )
    grad_normed_rel = dot(weight_in, grad_linear, CONTRACT_LAST)
    grad_normed_one = to_mesh_order(grad_normed_rel.reshape(devices, own_rows, rows))
    grad_normed_one = grad_normed_one.reshape(width, rows).T
    extra_one, grad_pre_att = pull_one(grad_normed_one)
    grad_inputs = grad_residual + extra_one
    grad_weight_in = dot(normed_rel, grad_linear).reshape(devices, own_rows, span)
    gain_grads = jnp.concatenate(
        [
            g.reshape(devices, -1)
            for g in (
                grad_pre_att,
                grad_post_att,
                grad_pre_fwd,
                grad_post_fwd,
                grad_query_gain,
                grad_key_gain,
            )
        ],
        axis=1,
    )
    gain_grads = to_relative(gain_grads)[:, None, :]
    gain_grads = jnp.pad(gain_grads, ((0, 0), (0, 7), (0, span - gain_grads.shape[2])))
    owned_in = rep_sum(scatter_sum(jnp.concatenate([grad_weight_in, gain_grads], axis=1)))
    owned_gains = owned_in[own_rows]
    owned_in = owned_in[:own_rows]
    ends = [k * own_rows for k in range(5)] + [4 * own_rows + own_gain, 4 * own_rows + 2 * own_gain]
    return (
        output,
        grad_inputs,
        *(owned_gains[a:b] for a, b in zip(ends[:-1], ends[1:])),
        owned_in[:, :features],
        owned_in[:, features : features + head_size],
        owned_in[:, features + head_size :],
        owned_output,
        owned_rows[:, :width],
        owned_rows[:, width : 2 * width],
        owned_rows[:, 2 * width :],
    )


def solution(mesh):
    tokens, weight, vector = (P(("rep", "fsdp"), None), P("fsdp", None), P("fsdp"))
    return jax.shard_map(
        local,
        mesh=mesh,
        in_specs=(tokens, P("rep", None), tokens) + (vector,) * 6 + (weight,) * 7,
        out_specs=(tokens, tokens) + (vector,) * 6 + (weight,) * 7,
        check_vma=False,
    )
```

```python
import functools
import math

import jax
import jax.numpy as jnp
from jax import lax
from jax.experimental import pallas as pl
from jax.experimental.pallas import tpu as pltpu
from jax.sharding import PartitionSpec as P

WINDOW = 512
EPSILON = 1e-06
MASKED = -1e30
CONTRACT_LAST = (((1,), (1,)), ((), ()))
CONTRACT_FIRST = (((0,), (0,)), ((), ()))
F32 = jnp.float32
LOW = jnp.bfloat16
NZ, NH, NC = (4, 2, 2)
GAIN_LINES = 8
NX = 2
PEERS = [(1, 0), (3, 0), (0, 1), (1, 1), (3, 1), (2, 0), (2, 1)]
NEAR = [(0, 0), (0, 1), (1, 0), (3, 0)]
FAR = [(1, 1), (3, 1), (2, 0), (2, 1)]
TILE = 256
ROW_GRANULE = 64
VMEM = 44 * 2**20


def place(z, h, c):
    return (z % NZ * NH + h % NH) * NC + c % NC


def route(dz, dh, dc):
    return [
        (place(z + dz, h + dh, c + dc), place(z, h, c))
        for z in range(NZ)
        for h in range(NH)
        for c in range(NC)
    ]


def fetch(block, dz, dh, dc=0):
    return lax.ppermute(block, "fsdp", route(dz, dh, dc))


def hand(block, dz, dh, dc=0):
    return fetch(block, -dz, -dh, -dc)


def swap(block):
    return fetch(block, 0, 0, 1)


def gather_chips(block):
    rows = block.shape[0]
    half = rows // 2
    pair = fetch(block, 0, 1)
    up, down = (fetch(block, 1, 0), fetch(block, 3, 0))
    above = fetch(jnp.concatenate([pair, up[:half]], axis=0), 1, 0)
    below = fetch(jnp.concatenate([pair, down[half:]], axis=0), 3, 0)
    last = (fetch(above[:half], 1, 0), fetch(below[half:rows], 3, 0))
    return {
        (0, 0): [block],
        (0, 1): [pair],
        (1, 0): [up],
        (3, 0): [down],
        (1, 1): [above[:rows]],
        (3, 1): [below[:rows]],
        (2, 0): [above[rows:], below[rows:]],
        (2, 1): list(last),
    }


def coordinates():
    me = lax.axis_index("fsdp")
    return (me // (NH * NC), me // NC % NH, me % NC)


def turned(blocks, start):
    twice = jnp.concatenate([blocks, blocks], axis=0)
    return lax.dynamic_slice_in_dim(twice, start, NZ, 0)


def flipped(blocks, amount, axis):
    return jnp.where(amount == 0, blocks, jnp.flip(blocks, axis))


def to_relative(lines):
    z, h, c = coordinates()
    blocks = lines.reshape(NZ, NH, NC, -1, *lines.shape[1:])
    return flipped(flipped(turned(blocks, z), h, 1), c, 2).reshape(lines.shape)


def to_mesh_order(lines):
    z, h, c = coordinates()
    blocks = lines.reshape(NZ, NH, NC, -1, *lines.shape[1:])
    return flipped(flipped(turned(blocks, (NZ - z) % NZ), h, 1), c, 2).reshape(lines.shape)


def in_offset_order(chips):
    mine = jnp.stack(
        [jnp.concatenate(chips[z, h], axis=0) for z in range(NZ) for h in range(NH)]
    )
    other = swap(mine)
    both = jnp.stack([mine, other], axis=1)
    return both.reshape(NZ * NH * NC, *mine.shape[1:])


def handed(offsets, values):
    rows = values.shape[0] // len(offsets)
    arrived = []
    for k, p in enumerate(offsets):
        block = values[k * rows : (k + 1) * rows]
        arrived.append(block if p == (0, 0) else hand(block, *p))
    return arrived


def sum_of(lists):
    total = None
    for arrived in lists:
        for block in arrived:
            total = block.astype(F32) if total is None else total + block.astype(F32)
    return total


def scatter_sum(blocks):
    chips = blocks.reshape(NZ, NH, NC, *blocks.shape[1:])
    away = swap(chips[:, :, 1].astype(LOW))
    both = chips[:, :, 0].astype(F32) + away.astype(F32)
    low = both.astype(LOW)
    total = both[0]
    for z in (1, 3, 2):
        total = total + hand(low[z], z, 0).astype(F32)
    return total[0] + hand(total[1].astype(LOW), 0, 1).astype(F32)


def y_groups():
    size = lax.axis_size("rep")
    return [list(range(x, size, NX)) for x in range(NX)]


def y_part(x):
    lines = x.reshape(lax.axis_size("rep") // NX, -1, x.shape[1])
    arrived = lax.all_to_all(
        lines, "rep", split_axis=0, concat_axis=0, tiled=True, axis_index_groups=y_groups()
    )
    return jnp.sum(arrived.astype(F32), axis=0)


def x_sum(x):
    pairs = [(r, r ^ 1) for r in range(lax.axis_size("rep"))]
    low = x.astype(LOW)
    return (low.astype(F32) + lax.ppermute(low, "rep", pairs).astype(F32)).astype(LOW)


def y_whole(part):
    copies = jnp.broadcast_to(part, (lax.axis_size("rep") // NX, *part.shape))
    whole = lax.all_to_all(
        copies, "rep", split_axis=0, concat_axis=0, tiled=True, axis_index_groups=y_groups()
    )
    return whole.reshape(-1, part.shape[1]).astype(F32)


def rep_part(x):
    parts = lax.axis_size("rep")
    lines = x.reshape(parts, -1, x.shape[1])
    arrived = lax.all_to_all(lines, "rep", split_axis=0, concat_axis=0, tiled=True)
    return jnp.sum(arrived.astype(F32), axis=0).astype(LOW)


def rep_whole(part):
    copies = jnp.broadcast_to(part, (lax.axis_size("rep"), *part.shape))
    whole = lax.all_to_all(copies, "rep", split_axis=0, concat_axis=0, tiled=True)
    return whole.reshape(-1, part.shape[1]).astype(F32)


def shifted(block, axis, distance):
    devices = range(lax.axis_size(axis))
    pairs = [(i - distance, i) for i in devices if i - distance in devices]
    return lax.ppermute(block, axis, pairs)


def norm_rows(values, gain):
    return values * lax.rsqrt(jnp.mean(values * values, axis=-1, keepdims=True) + EPSILON) * gain


def rotate(values, position):
    half = values.shape[-1] // 2
    freq = 10000.0 ** (-2.0 * jnp.arange(half, dtype=F32) / values.shape[-1])
    angle = position.astype(F32)[:, None] * freq[None, :]
    cosine = jnp.cos(angle)[:, None, :]
    sine = jnp.sin(angle)[:, None, :]
    first = values[..., :half]
    second = values[..., half:]
    return jnp.concatenate(
        [first * cosine - second * sine, second * cosine + first * sine], axis=-1
    )


def doc_info(lengths, index):
    ends = jnp.cumsum(lengths)
    starts = ends - lengths
    segment = jnp.sum((index[:, None] >= ends[None, :-1]).astype(jnp.int32), axis=1)
    hit = segment[:, None] == jnp.arange(lengths.shape[0], dtype=jnp.int32)[None, :]
    first = jnp.sum(jnp.where(hit, starts[None, :], 0), axis=1)
    segment = jnp.where(index < 0, -1, segment)
    return (segment, index - first)


def dot(a, b, dims=(((1,), (0,)), ((), ()))):
    return lax.dot_general(a, b, dims, preferred_element_type=F32)


GELU_SCALE = math.sqrt(2.0 / math.pi)
GELU_CUBE = 0.044715


def join(pieces, whole):
    at = 0
    for piece in pieces:
        whole[at : at + piece.shape[0], :] = piece[...]
        at += piece.shape[0]


def feed_kernel(count, *refs):
    pieces, weights, (x, *saved, out) = (refs[:count], refs[count : count + 6], refs[count + 6 :])
    join(pieces, x)

    @pl.loop(0, x.shape[0] // TILE)
    def _(step):
        lines = pl.ds(pl.multiple_of(step * TILE, TILE), TILE)
        block = x[lines, :]
        total = None
        for half in range(2):
            gate_w, up_w, down_w = weights[half::2]
            gate_s, up_s, hidden_s = saved[half::2]
            gate = dot(block, gate_w[...], CONTRACT_LAST)
            upward = dot(block, up_w[...], CONTRACT_LAST)
            bend = jnp.tanh(GELU_SCALE * (gate + GELU_CUBE * gate * gate * gate))
            hidden = (0.5 * gate * (1.0 + bend) * upward).astype(LOW)
            gate_s[lines, :] = gate.astype(LOW)
            up_s[lines, :] = upward.astype(LOW)
            hidden_s[lines, :] = hidden
            part = dot(hidden, down_w[...])
            total = part if total is None else total + part
        out[lines, :] = total.astype(LOW)


def back_kernel(count, *refs):
    pieces, weights = (refs[:count], refs[count : count + 6])
    gates, ups = (refs[count + 6 : count + 8], refs[count + 8 : count + 10])
    grad, *saved, out = refs[count + 10 :]
    join(pieces, grad)

    @pl.loop(0, grad.shape[0] // TILE)
    def _(step):
        lines = pl.ds(pl.multiple_of(step * TILE, TILE), TILE)
        block = grad[lines, :]
        total = None
        for half in range(2):
            gate_w, up_w, down_w = weights[half::2]
            grad_hidden = dot(block, down_w[...], CONTRACT_LAST)
            gate = gates[half][lines, :].astype(F32)
            upward = ups[half][lines, :].astype(F32)
            square = gate * gate
            bend = jnp.tanh(GELU_SCALE * gate * (1.0 + GELU_CUBE * square))
            rise = 0.5 * (1.0 + bend)
            slope = rise + 0.5 * gate * (1.0 - bend * bend) * (
                GELU_SCALE * (1.0 + 3.0 * GELU_CUBE * square)
            )
            grad_gate = (grad_hidden * upward * slope).astype(LOW)
            grad_up = (grad_hidden * gate * rise).astype(LOW)
            saved[half][lines, :] = grad_gate
            saved[2 + half][lines, :] = grad_up
            part = dot(grad_gate, gate_w[...]) + dot(grad_up, up_w[...])
            total = part if total is None else total + part
        out[lines, :] = total.astype(LOW)


def rows_kernel(add, *refs):
    x, grad, gates, ups, hiddens = (refs[k : k + 2] for k in range(0, 10, 2))
    out = refs[-1]
    hidden, width = (gates[0].shape[1], x[0].shape[1])
    for k, (left, right) in enumerate(((gates, x), (ups, x), (hiddens, grad))):
        columns = slice(k * width, (k + 1) * width)
        total = dot(left[0][...], right[0][...], CONTRACT_FIRST)
        total = total + dot(left[1][...], right[1][...], CONTRACT_FIRST)
        if add:
            total = total + refs[10][:hidden, columns].astype(F32)
        out[:hidden, columns] = total.astype(LOW)
    out[hidden:, :] = jnp.zeros((out.shape[0] - hidden, out.shape[1]), LOW)


def whole_call(kernel, shapes, flops, args):
    moved = sum(math.prod(a.shape) * 2 for a in (*args, *shapes))
    return pl.pallas_call(
        kernel,
        out_shape=shapes,
        in_specs=[pl.BlockSpec(memory_space=pltpu.VMEM)] * len(args),
        out_specs=[pl.BlockSpec(memory_space=pltpu.VMEM)] * len(shapes),
        compiler_params=pltpu.CompilerParams(vmem_limit_bytes=VMEM),
        cost_estimate=pl.CostEstimate(flops=flops, bytes_accessed=moved, transcendentals=0),
    )(*args)


def feed(pieces, weights):
    rows, (hidden, width) = (sum(p.shape[0] for p in pieces), weights[0].shape)
    shapes = [jax.ShapeDtypeStruct((rows, n), LOW) for n in [width] + [hidden] * 6 + [width]]
    return whole_call(
        functools.partial(feed_kernel, len(pieces)),
        shapes,
        12 * rows * hidden * width,
        (*pieces, *weights),
    )


def feed_back(pieces, weights, gates, ups):
    rows, (hidden, width) = (sum(p.shape[0] for p in pieces), weights[0].shape)
    shapes = [jax.ShapeDtypeStruct((rows, n), LOW) for n in [width] + [hidden] * 4 + [width]]
    return whole_call(
        functools.partial(back_kernel, len(pieces)),
        shapes,
        12 * rows * hidden * width,
        (*pieces, *weights, *gates, *ups),
    )


def row_gradients(chunks, added):
    args = [a for both in chunks for a in both]
    rows, width = args[0].shape
    hidden = args[4].shape[1]
    lines = hidden + -hidden % ROW_GRANULE
    shapes = [jax.ShapeDtypeStruct((lines, 3 * width), LOW)]
    more = [] if added is None else [added]
    return whole_call(
        functools.partial(rows_kernel, added is not None),
        shapes,
        12 * rows * hidden * width,
        (*args, *more),
    )[0]


def local(
    tokens,
    lengths,
    cotangent,
    pre_attention,
    post_attention,
    pre_forward,
    post_forward,
    query_gain,
    key_gain,
    query_weight,
    key_weight,
    value_weight,
    output_weight,
    gate_rows,
    up_rows,
    down_rows,
):
    rows = tokens.shape[0]
    width = tokens.shape[1]
    head_size = key_weight.shape[1]
    heads = query_weight.shape[1] // head_size
    features = heads * head_size
    span = features + 2 * head_size
    devices = NZ * NH * NC
    own_rows = query_weight.shape[0]
    own_gain = query_gain.shape[0]
    chips_back = (WINDOW + NC * rows - 1) // (NC * rows)
    shard = lax.axis_index("fsdp")
    local_index = shard * rows + jnp.arange(rows, dtype=jnp.int32)
    other = shard + 1 - 2 * (shard % NC)
    key_index = jnp.concatenate(
        [
            (core - back * NC) * rows + jnp.arange(rows, dtype=jnp.int32)
            for core in (shard, other)
            for back in range(chips_back, -1, -1)
        ]
    )
    query_seg, query_pos = doc_info(lengths[0], local_index)
    key_seg, key_place = doc_info(lengths[0], key_index)
    distance = local_index[:, None] - key_index[None, :]
    allowed = (query_seg[:, None] == key_seg[None, :]) & (distance >= 0) & (distance < WINDOW)

    gains = (pre_attention, post_attention, pre_forward, post_forward, query_gain, key_gain)
    lines = [jnp.pad(g[None, :], ((0, 0), (0, span - g.shape[0]))) for g in gains]
    packed = jnp.concatenate(
        [
            jnp.concatenate([query_weight, key_weight, value_weight], axis=1),
            *lines,
            jnp.zeros((GAIN_LINES - len(lines), span), LOW),
        ],
        axis=0,
    )
    weight_out = lax.all_gather(output_weight, "fsdp", axis=0, tiled=True)
    first_all = in_offset_order(gather_chips(packed))
    weight_in = first_all[:, :own_rows].reshape(width, span)
    gain_all = to_mesh_order(first_all[:, own_rows:, :own_rows]).astype(F32)
    gain_pre_att, gain_post_att, gain_pre_fwd, gain_post_fwd = (
        gain_all[:, k].reshape(width) for k in range(4)
    )
    gain_query, gain_key = (gain_all[:, 4 + k, :own_gain].reshape(head_size) for k in range(2))
    feed_weights = [w for own in (gate_rows, up_rows, down_rows) for w in (own, swap(own))]

    inputs = tokens.astype(F32)
    normed_one, pull_one = jax.vjp(norm_rows, inputs, gain_pre_att)
    normed_low = normed_one.astype(LOW)
    normed_rel = to_relative(normed_low.T.reshape(devices, own_rows, rows)).reshape(width, rows)
    linear = dot(normed_rel, weight_in, CONTRACT_FIRST)
    query_lin = linear[:, :features]
    key_lin = linear[:, features : features + head_size]
    value_low = linear[:, features + head_size :].astype(LOW)

    def query_side(lin, gain):
        return rotate(
            norm_rows(lin.reshape(rows, heads, head_size), gain), query_pos
        ) * head_size ** (-0.5)

    def key_side(lin, gain):
        return rotate(norm_rows(lin[:, None, :], gain), query_pos)[:, 0, :]

    query_value, pull_query = jax.vjp(query_side, query_lin, gain_query)
    key_value, pull_key = jax.vjp(key_side, key_lin, gain_key)
    query_low = query_value.astype(LOW)
    key_low = key_value.astype(LOW)
    outgoing = jnp.concatenate([key_low, value_low], axis=1)
    arrived = [shifted(outgoing, "fsdp", NC * back) for back in range(chips_back, 0, -1)]
    mine = jnp.concatenate(arrived + [outgoing], axis=0)
    both = jnp.concatenate([mine, swap(mine)], axis=0)
    keys_all = both[:, :head_size]
    values_all = both[:, head_size:]
    scores = jnp.einsum("thd,kd->htk", query_low, keys_all, preferred_element_type=F32)
    scores = jnp.where(allowed[None], scores, MASKED)
    peak = jnp.max(scores, axis=-1, keepdims=True)
    expo = jnp.exp(scores - peak)
    total = jnp.sum(expo, axis=-1, keepdims=True)
    probs = expo / total
    probs_low = probs.astype(LOW)
    mixed = jnp.einsum("htk,kd->thd", probs_low, values_all, preferred_element_type=F32)
    mixed_low = mixed.reshape(rows, features).astype(LOW)
    mixed_rel = to_relative(mixed_low.T.reshape(devices, -1, rows)).reshape(features, rows)
    projected = dot(mixed_low, weight_out)
    attended, pull_two = jax.vjp(norm_rows, projected, gain_post_att)
    residual_one = inputs + attended
    normed_two, pull_three = jax.vjp(norm_rows, residual_one, gain_pre_fwd)
    normed_two_low = normed_two.astype(LOW)

    normed_of = gather_chips(normed_two_low)
    acts, sent = ([], [])
    for offsets in (NEAR, FAR):
        pieces = [piece for p in offsets for piece in normed_of[p]]
        *kept, down = feed(pieces, feed_weights)
        acts.append(kept)
        sent.append(handed(offsets, down))
    down_sum = sum_of(sent)
    fed, pull_four = jax.vjp(norm_rows, down_sum, gain_post_fwd)
    output = (residual_one + fed).astype(LOW)
    grad_out = cotangent.astype(F32)
    grad_down, grad_post_fwd = pull_four(grad_out)
    grad_down_of = gather_chips(grad_down.astype(LOW))
    backs, sent = ([], [])
    for offsets, kept in zip((NEAR, FAR), acts):
        pieces = [piece for p in offsets for piece in grad_down_of[p]]
        *grads, back = feed_back(pieces, feed_weights, kept[1:3], kept[3:5])
        backs.append(grads)
        sent.append(handed(offsets, back))
    grad_normed_two = sum_of(sent)
    products = [
        [
            [kept[0] for kept in acts],
            [grads[0] for grads in backs],
            [grads[1 + half] for grads in backs],
            [grads[3 + half] for grads in backs],
            [kept[5 + half] for kept in acts],
        ]
        for half in range(2)
    ]
    hidden_rows = gate_rows.shape[0]
    owned_rows = row_gradients(products[0], swap(row_gradients(products[1], None)))
    grad_normed_two, owned_rows = lax.optimization_barrier((grad_normed_two, owned_rows))
    rows_part = y_part(owned_rows)

    extra_three, grad_pre_fwd = pull_three(grad_normed_two)
    grad_residual = grad_out + extra_three
    grad_projected, grad_post_att = pull_two(grad_residual)
    grad_proj_low = grad_projected.astype(LOW)
    grad_mixed_low = dot(grad_proj_low, weight_out, CONTRACT_LAST).astype(LOW)
    grad_output_weight = dot(mixed_rel, grad_proj_low).reshape(devices, -1, width)
    output_part = scatter_sum(grad_output_weight)
    grad_mixed_heads = grad_mixed_low.reshape(rows, heads, head_size)
    grad_probs = jnp.einsum("thd,kd->htk", grad_mixed_heads, values_all, preferred_element_type=F32)
    inner = jnp.sum(grad_probs * probs, axis=-1, keepdims=True)
    grad_scores = (probs * (grad_probs - inner)).astype(LOW)
    grad_query_low = jnp.einsum(
        "htk,kd->thd", grad_scores, keys_all, preferred_element_type=F32
    ).astype(LOW)
    grad_keys_all = jnp.einsum("htk,thd->kd", grad_scores, query_low, preferred_element_type=F32)
    grad_values_all = jnp.einsum(
        "htk,thd->kd", probs_low, grad_mixed_heads, preferred_element_type=F32
    )
    grad_both = jnp.concatenate([grad_keys_all, grad_values_all], axis=1)
    half = (chips_back + 1) * rows
    grad_both = grad_both[:half] + swap(grad_both[half:].astype(LOW)).astype(F32)
    owned_both = grad_both[chips_back * rows :]
    for back in range(1, chips_back + 1):
        piece = grad_both[(chips_back - back) * rows : (chips_back - back + 1) * rows]
        owned_both = owned_both + shifted(piece.astype(LOW), "fsdp", -NC * back).astype(F32)
    owned_both, rows_part = lax.optimization_barrier((owned_both, rows_part))
    rows_part = x_sum(rows_part)
    grad_key_low = owned_both[:, :head_size].astype(LOW)
    grad_value_low = owned_both[:, head_size:].astype(LOW)
    grad_query_lin, grad_query_gain = pull_query(grad_query_low.astype(F32))
    grad_key_lin, grad_key_gain = pull_key(grad_key_low.astype(F32))
    grad_linear = jnp.concatenate(
        [grad_query_lin.astype(LOW), grad_key_lin.astype(LOW), grad_value_low], axis=1
    )
    grad_normed_rel = dot(weight_in, grad_linear, CONTRACT_LAST)
    grad_normed_one = to_mesh_order(grad_normed_rel.reshape(devices, own_rows, rows))
    grad_normed_one = grad_normed_one.reshape(width, rows).T
    extra_one, grad_pre_att = pull_one(grad_normed_one)
    grad_inputs = grad_residual + extra_one
    grad_weight_in = dot(normed_rel, grad_linear).reshape(devices, own_rows, span)
    gain_grads = jnp.stack(
        [
            jnp.pad(g.reshape(devices, -1), ((0, 0), (0, own_rows - g.shape[0] // devices)))
            for g in (
                grad_pre_att,
                grad_post_att,
                grad_pre_fwd,
                grad_post_fwd,
                grad_query_gain,
                grad_key_gain,
            )
        ],
        axis=1,
    )
    gain_grads = to_relative(gain_grads)
    gain_grads = jnp.pad(
        gain_grads, ((0, 0), (0, GAIN_LINES - gain_grads.shape[1]), (0, span - own_rows))
    )
    all_in = jnp.concatenate([grad_weight_in, gain_grads], axis=1)
    all_in, output_part, rows_part = lax.optimization_barrier((all_in, output_part, rows_part))
    in_part = scatter_sum(all_in)
    owned_rows = y_whole(rows_part)
    cut = output_part.shape[0] * width // span
    third = jnp.split(output_part[cut:, :], width // (span - width), axis=1)
    output_lines = jnp.concatenate([output_part[:cut], jnp.concatenate(third, axis=0)], axis=1)
    share = jnp.concatenate([in_part, output_lines], axis=0).astype(LOW)
    share, owned_rows = lax.optimization_barrier((share, owned_rows))
    owned_rows = owned_rows[:hidden_rows]
    owned_in = rep_whole(rep_part(share))
    output_lines = owned_in[in_part.shape[0] :]
    third = jnp.split(output_lines[:, width:], width // (span - width), axis=0)
    owned_output = jnp.concatenate(
        [output_lines[:, :width], jnp.concatenate(third, axis=1)], axis=0
    )
    owned_gains = [owned_in[own_rows + k, :own_rows] for k in range(4)]
    owned_gains += [owned_in[own_rows + 4 + k, :own_gain] for k in range(2)]
    owned_in = owned_in[:own_rows]
    return (
        output,
        grad_inputs,
        *owned_gains,
        owned_in[:, :features],
        owned_in[:, features : features + head_size],
        owned_in[:, features + head_size :],
        owned_output,
        owned_rows[:, :width],
        owned_rows[:, width : 2 * width],
        owned_rows[:, 2 * width :],
    )


def solution(mesh):
    tokens, weight, vector = (P(("rep", "fsdp"), None), P("fsdp", None), P("fsdp"))
    return jax.shard_map(
        local,
        mesh=mesh,
        in_specs=(tokens, P("rep", None), tokens) + (vector,) * 6 + (weight,) * 7,
        out_specs=(tokens, tokens) + (vector,) * 6 + (weight,) * 7,
        check_vma=False,
    )
```

```python
import functools
import math

import jax
import jax.numpy as jnp
from jax import lax
from jax.experimental import pallas as pl
from jax.experimental.pallas import tpu as pltpu
from jax.sharding import PartitionSpec as P

WINDOW = 512
EPSILON = 1e-06
MASKED = -1e30
CONTRACT_LAST = (((1,), (1,)), ((), ()))
CONTRACT_FIRST = (((0,), (0,)), ((), ()))
F32 = jnp.float32
LOW = jnp.bfloat16
NZ, NH, NC = (4, 2, 2)
GAIN_LINES = 8
NY, NX = (4, 2)
PEERS = [(1, 0), (3, 0), (0, 1), (1, 1), (3, 1), (2, 0), (2, 1)]
NEAR = [(0, 0), (0, 1), (1, 0), (3, 0)]
FAR = [(1, 1), (3, 1), (2, 0), (2, 1)]
TILE = 256
ROW_GRANULE = 64
VMEM = 44 * 2**20


def place(z, h, c):
    return (z % NZ * NH + h % NH) * NC + c % NC


def route(dz, dh, dc):
    return [
        (place(z + dz, h + dh, c + dc), place(z, h, c))
        for z in range(NZ)
        for h in range(NH)
        for c in range(NC)
    ]


def fetch(block, dz, dh, dc=0):
    return lax.ppermute(block, "fsdp", route(dz, dh, dc))


def hand(block, dz, dh, dc=0):
    return fetch(block, -dz, -dh, -dc)


def swap(block):
    return fetch(block, 0, 0, 1)


def gather_chips(block):
    rows = block.shape[0]
    half = rows // 2
    pair = fetch(block, 0, 1)
    up, down = (fetch(block, 1, 0), fetch(block, 3, 0))
    above = fetch(jnp.concatenate([pair, up[:half]], axis=0), 1, 0)
    below = fetch(jnp.concatenate([pair, down[half:]], axis=0), 3, 0)
    last = (fetch(above[:half], 1, 0), fetch(below[half:rows], 3, 0))
    return {
        (0, 0): [block],
        (0, 1): [pair],
        (1, 0): [up],
        (3, 0): [down],
        (1, 1): [above[:rows]],
        (3, 1): [below[:rows]],
        (2, 0): [above[rows:], below[rows:]],
        (2, 1): list(last),
    }


def coordinates():
    me = lax.axis_index("fsdp")
    return (me // (NH * NC), me // NC % NH, me % NC)


def turned(blocks, start):
    twice = jnp.concatenate([blocks, blocks], axis=0)
    return lax.dynamic_slice_in_dim(twice, start, NZ, 0)


def flipped(blocks, amount, axis):
    return jnp.where(amount == 0, blocks, jnp.flip(blocks, axis))


def to_relative(lines):
    z, h, c = coordinates()
    blocks = lines.reshape(NZ, NH, NC, -1, *lines.shape[1:])
    return flipped(flipped(turned(blocks, z), h, 1), c, 2).reshape(lines.shape)


def to_mesh_order(lines):
    z, h, c = coordinates()
    blocks = lines.reshape(NZ, NH, NC, -1, *lines.shape[1:])
    return flipped(flipped(turned(blocks, (NZ - z) % NZ), h, 1), c, 2).reshape(lines.shape)


def in_offset_order(chips, after):
    mine = jnp.stack(
        [jnp.concatenate(chips[z, h], axis=0) for z in range(NZ) for h in range(NH)]
    )
    mine, after = lax.optimization_barrier((mine, after))
    other = swap(mine)
    both = jnp.stack([mine, other], axis=1)
    return both.reshape(NZ * NH * NC, *mine.shape[1:]), after


def handed(offsets, values):
    rows = values.shape[0] // len(offsets)
    arrived = []
    for k, p in enumerate(offsets):
        block = values[k * rows : (k + 1) * rows]
        arrived.append(block if p == (0, 0) else hand(block, *p))
    return arrived


def sum_of(lists):
    total = None
    for arrived in lists:
        for block in arrived:
            total = block.astype(F32) if total is None else total + block.astype(F32)
    return total


def unfolded(lines, width):
    columns = lines.shape[1]
    count = lines.shape[0] * columns // width
    rest = jnp.split(lines[count:], columns // (width - columns), axis=1)
    return jnp.concatenate([lines[:count], jnp.concatenate(rest, axis=0)], axis=1)


def chip_sums(mine, away):
    total = (mine.astype(F32) + swap(away).astype(F32)).astype(LOW)
    return total.reshape(NZ, NH, -1, mine.shape[1])


def z_sums(low):
    total = low[0].astype(F32)
    for z in (1, 3, 2):
        total = total + hand(low[z], z, 0).astype(F32)
    return total


def pair_sum(total):
    return total[0] + hand(total[1].astype(LOW), 0, 1).astype(F32)


def rep_fetch(block, dy, dx=0):
    size = lax.axis_size("rep")
    pairs = [
        ((y + dy) % (size // NX) * NX + (x + dx) % NX, y * NX + x)
        for y in range(size // NX)
        for x in range(NX)
    ]
    return lax.ppermute(block, "rep", pairs)


def lines_of(x, dy):
    number = lax.axis_size("rep") // NX
    size = x.shape[0] // number
    at = (lax.axis_index("rep") // NX + dy) % number * size
    return lax.dynamic_slice_in_dim(x, at, size, 0)


def y_groups():
    size = lax.axis_size("rep")
    return [list(range(x, size, NX)) for x in range(NX)]


def y_part(x):
    lines = x.reshape(lax.axis_size("rep") // NX, -1, x.shape[1])
    arrived = lax.all_to_all(
        lines, "rep", split_axis=0, concat_axis=0, tiled=True, axis_index_groups=y_groups()
    )
    return jnp.sum(arrived.astype(F32), axis=0)


def x_sum(x):
    low = x.astype(LOW)
    return (low.astype(F32) + rep_fetch(low, 0, 1).astype(F32)).astype(LOW)


def placed(pieces):
    size = sum(values.shape[0] for dy, at, values in pieces) // NY
    whole = jnp.zeros((size * NY, pieces[0][2].shape[1]), LOW)
    y = lax.axis_index("rep") // NX
    for dy, at, values in pieces:
        whole = lax.dynamic_update_slice(whole, values, ((y + dy) % NY * size + at, 0))
    return whole


def y_whole(part):
    copies = jnp.broadcast_to(part, (NY, *part.shape))
    whole = lax.all_to_all(
        copies, "rep", split_axis=0, concat_axis=0, tiled=True, axis_index_groups=y_groups()
    )
    return whole.reshape(-1, part.shape[1])


def rep_sum(x, after):
    arrived = [rep_fetch(lines_of(x, -dy), dy) for dy in (1, 3, 2)]
    part = lines_of(x, 0).astype(F32)
    for block in arrived:
        part = part + block.astype(F32)
    part, after = lax.optimization_barrier((x_sum(part), after))
    total = placed([(0, 0, part)] + [(dy, 0, rep_fetch(part, dy)) for dy in (1, 3, 2)])
    return total.astype(F32), after


def shifted(block, axis, distance):
    devices = range(lax.axis_size(axis))
    pairs = [(i - distance, i) for i in devices if i - distance in devices]
    return lax.ppermute(block, axis, pairs)


def norm_rows(values, gain):
    return values * lax.rsqrt(jnp.mean(values * values, axis=-1, keepdims=True) + EPSILON) * gain


def rope_table(position, size):
    half = size // 2
    freq = 10000.0 ** (-2.0 * jnp.arange(half, dtype=F32) / size)
    angle = position.astype(F32)[:, None] * freq[None, :]
    return jnp.cos(angle), jnp.sin(angle)


def rotate(values, table):
    half = values.shape[-1] // 2
    cosine, sine = (part[:, None, :] for part in table)
    first = values[..., :half]
    second = values[..., half:]
    return jnp.concatenate(
        [first * cosine - second * sine, second * cosine + first * sine], axis=-1
    )


def doc_info(lengths, index):
    ends = jnp.cumsum(lengths)
    starts = ends - lengths
    segment = jnp.sum((index[:, None] >= ends[None, :-1]).astype(jnp.int32), axis=1)
    hit = segment[:, None] == jnp.arange(lengths.shape[0], dtype=jnp.int32)[None, :]
    first = jnp.sum(jnp.where(hit, starts[None, :], 0), axis=1)
    segment = jnp.where(index < 0, -1, segment)
    return (segment, index - first)


def dot(a, b, dims=(((1,), (0,)), ((), ()))):
    return lax.dot_general(a, b, dims, preferred_element_type=F32)


GELU_SCALE = math.sqrt(2.0 / math.pi)
GELU_CUBE = 0.044715


def join(pieces, whole):
    at = 0
    for piece in pieces:
        whole[at : at + piece.shape[0], :] = piece[...]
        at += piece.shape[0]


def feed_kernel(count, *refs):
    pieces, weights, (x, *saved, out) = (refs[:count], refs[count : count + 6], refs[count + 6 :])
    join(pieces, x)

    @pl.loop(0, x.shape[0] // TILE)
    def _(step):
        lines = pl.ds(pl.multiple_of(step * TILE, TILE), TILE)
        block = x[lines, :]
        total = None
        for half in range(2):
            gate_w, up_w, down_w = weights[half::2]
            gate_s, up_s, hidden_s = saved[half::2]
            gate = dot(block, gate_w[...], CONTRACT_LAST)
            upward = dot(block, up_w[...], CONTRACT_LAST)
            bend = jnp.tanh(GELU_SCALE * (gate + GELU_CUBE * gate * gate * gate))
            hidden = (0.5 * gate * (1.0 + bend) * upward).astype(LOW)
            gate_s[lines, :] = gate.astype(LOW)
            up_s[lines, :] = upward.astype(LOW)
            hidden_s[lines, :] = hidden
            part = dot(hidden, down_w[...])
            total = part if total is None else total + part
        out[lines, :] = total.astype(LOW)


def back_kernel(count, *refs):
    pieces, weights = (refs[:count], refs[count : count + 6])
    gates, ups = (refs[count + 6 : count + 8], refs[count + 8 : count + 10])
    grad, *saved, out = refs[count + 10 :]
    join(pieces, grad)

    @pl.loop(0, grad.shape[0] // TILE)
    def _(step):
        lines = pl.ds(pl.multiple_of(step * TILE, TILE), TILE)
        block = grad[lines, :]
        total = None
        for half in range(2):
            gate_w, up_w, down_w = weights[half::2]
            grad_hidden = dot(block, down_w[...], CONTRACT_LAST)
            gate = gates[half][lines, :].astype(F32)
            upward = ups[half][lines, :].astype(F32)
            square = gate * gate
            bend = jnp.tanh(GELU_SCALE * gate * (1.0 + GELU_CUBE * square))
            rise = 0.5 * (1.0 + bend)
            slope = rise + 0.5 * gate * (1.0 - bend * bend) * (
                GELU_SCALE * (1.0 + 3.0 * GELU_CUBE * square)
            )
            grad_gate = (grad_hidden * upward * slope).astype(LOW)
            grad_up = (grad_hidden * gate * rise).astype(LOW)
            saved[half][lines, :] = grad_gate
            saved[2 + half][lines, :] = grad_up
            part = dot(grad_gate, gate_w[...]) + dot(grad_up, up_w[...])
            total = part if total is None else total + part
        out[lines, :] = total.astype(LOW)


def rows_kernel(count, *refs):
    out = refs[-1]
    hidden, width = (refs[0].shape[1], refs[2].shape[1])
    for k in range(count):
        left, right = (refs[4 * k : 4 * k + 2], refs[4 * k + 2 : 4 * k + 4])
        columns = slice(k * width, (k + 1) * width)
        total = dot(left[0][...], right[0][...], CONTRACT_FIRST)
        total = total + dot(left[1][...], right[1][...], CONTRACT_FIRST)
        if len(refs) > 4 * count + 1:
            total = total + refs[4 * count][:hidden, columns].astype(F32)
        out[:hidden, columns] = total.astype(LOW)
    out[hidden:, :] = jnp.zeros((out.shape[0] - hidden, out.shape[1]), LOW)


def head_slices(queries, head_size):
    return [slice(at, at + head_size) for at in range(0, queries.shape[1], head_size)]


def masked_softmax(query, keys, mask):
    scores = jnp.where(mask > 0, dot(query, keys, CONTRACT_LAST), MASKED)
    expo = jnp.exp(scores - jnp.max(scores, axis=-1, keepdims=True))
    return expo / jnp.sum(expo, axis=-1, keepdims=True)


def attend_kernel(query, both, mask, weight, inputs, gains, mixed, projected, residual, normed):
    size = both.shape[1] // 2
    keys, values, allowed = (both[:, :size], both[:, size:], mask[...])
    for columns in head_slices(query, size):
        probs = masked_softmax(query[:, columns], keys, allowed)
        mixed[:, columns] = dot(probs.astype(LOW), values).astype(LOW)
    lines = dot(mixed[...], weight[...])
    projected[...] = lines
    lines = inputs[...].astype(F32) + norm_rows(lines, gains[0:1, :])
    residual[...] = lines
    normed[...] = norm_rows(lines, gains[1:2, :]).astype(LOW)


def attend_back_kernel(
    grad, weight, query, both, mask, linear, turns, gain, out, grad_gain, own, away, total
):
    size = both.shape[1] // 2
    half = size // 2
    keys, values, allowed = (both[:, :size], both[:, size:], mask[...])
    cosine, sine = (turns[:, :half], turns[:, half:])
    grad_gain[...] = jnp.zeros_like(grad_gain)
    for head, columns in enumerate(head_slices(query, size)):
        probs = masked_softmax(query[:, columns], keys, allowed)
        grad_mixed = dot(grad[...], weight[columns, :], CONTRACT_LAST).astype(LOW)
        grad_probs = dot(grad_mixed, values, CONTRACT_LAST)
        inner = jnp.sum(grad_probs * probs, axis=-1, keepdims=True)
        grad_scores = (probs * (grad_probs - inner)).astype(LOW)
        grad_keys = dot(grad_scores, query[:, columns], CONTRACT_FIRST)
        grad_values = dot(probs.astype(LOW), grad_mixed, CONTRACT_FIRST)
        if head == 0:
            total[:, :size] = grad_keys
            total[:, size:] = grad_values
        else:
            total[:, :size] += grad_keys
            total[:, size:] += grad_values
        turned_grad = dot(grad_scores, keys).astype(LOW).astype(F32) * size**-0.5
        first, second = (turned_grad[:, :half], turned_grad[:, half:])
        grad_normed = jnp.concatenate(
            [first * cosine + second * sine, second * cosine - first * sine], axis=1
        )
        lines = linear[:, columns]
        scale = lax.rsqrt(jnp.mean(lines * lines, axis=-1, keepdims=True) + EPSILON)
        grad_gain[0:1, :] += jnp.sum(grad_normed * lines * scale, axis=0, keepdims=True)
        grad_normed = grad_normed * gain[0:1, :]
        share = jnp.mean(grad_normed * lines, axis=-1, keepdims=True)
        out[:, columns] = (scale * grad_normed - lines * (scale * scale * scale * share)).astype(LOW)
    kept = own.shape[0]
    own[...] = total[:kept, :]
    away[...] = total[kept:, :].astype(LOW)


def wide_kernel(inputs, query, mixed, grad, mine, away, block):
    devices, columns = (mine.shape[0] * 2 // block.shape[0], query.shape[1])
    query_grad = dot(inputs[...], query[...])
    output_grad = dot(mixed[...], grad[...])
    own, lines = (query_grad.shape[0] // devices, output_grad.shape[0] // devices)
    rest = output_grad.shape[1] - columns
    size = lines * rest // columns
    for number in range(devices):
        part = output_grad[number * lines : (number + 1) * lines]
        block[:own, :] = query_grad[number * own : (number + 1) * own]
        block[own : own + lines, :] = part[:, :columns]
        for k in range(columns // rest):
            block[own + lines :, k * rest : (k + 1) * rest] = part[
                k * size : (k + 1) * size, columns:
            ]
        out = away if number % 2 else mine
        at = number // 2 * block.shape[0]
        out[at : at + block.shape[0], :] = block[...].astype(LOW)


def pair_kernel(inputs, pair, gains, mine, away, block):
    pair_grad = dot(inputs[...], pair[...])
    devices = mine.shape[0] * 2 // block.shape[0]
    own = pair_grad.shape[0] // devices
    more = block.shape[0] - own
    for number in range(devices):
        block[:own, :] = pair_grad[number * own : (number + 1) * own]
        block[own:, :] = gains[number * more : (number + 1) * more, :]
        out = away if number % 2 else mine
        at = number // 2 * block.shape[0]
        out[at : at + block.shape[0], :] = block[...].astype(LOW)


def block_call(kernel, lines, columns, args):
    half = jax.ShapeDtypeStruct((NZ * NH * lines, columns), LOW)
    flops = 4 * args[0].shape[0] * args[0].shape[1] * columns
    return whole_call(kernel, [half, half], flops, args, [pltpu.VMEM((lines, columns), F32)])


def whole_call(kernel, shapes, flops, args, scratch=()):
    moved = sum(math.prod(a.shape) * 2 for a in (*args, *shapes))
    return pl.pallas_call(
        kernel,
        out_shape=shapes,
        in_specs=[pl.BlockSpec(memory_space=pltpu.VMEM)] * len(args),
        out_specs=[pl.BlockSpec(memory_space=pltpu.VMEM)] * len(shapes),
        scratch_shapes=scratch,
        compiler_params=pltpu.CompilerParams(vmem_limit_bytes=VMEM),
        cost_estimate=pl.CostEstimate(flops=flops, bytes_accessed=moved, transcendentals=0),
    )(*args)


def feed(pieces, weights):
    rows, (hidden, width) = (sum(p.shape[0] for p in pieces), weights[0].shape)
    shapes = [jax.ShapeDtypeStruct((rows, n), LOW) for n in [width] + [hidden] * 6 + [width]]
    return whole_call(
        functools.partial(feed_kernel, len(pieces)),
        shapes,
        12 * rows * hidden * width,
        (*pieces, *weights),
    )


def feed_back(pieces, weights, gates, ups):
    rows, (hidden, width) = (sum(p.shape[0] for p in pieces), weights[0].shape)
    shapes = [jax.ShapeDtypeStruct((rows, n), LOW) for n in [width] + [hidden] * 4 + [width]]
    return whole_call(
        functools.partial(back_kernel, len(pieces)),
        shapes,
        12 * rows * hidden * width,
        (*pieces, *weights, *gates, *ups),
    )


def row_gradients(pairs, added=()):
    args = [a for left, right in pairs for a in (*left, *right)]
    rows, hidden = args[0].shape
    width = args[2].shape[1]
    lines = hidden + -hidden % ROW_GRANULE
    return whole_call(
        functools.partial(rows_kernel, len(pairs)),
        [jax.ShapeDtypeStruct((lines, len(pairs) * width), LOW)],
        4 * len(pairs) * rows * hidden * width,
        (*args, *added),
    )[0]


def local(
    tokens,
    lengths,
    cotangent,
    pre_attention,
    post_attention,
    pre_forward,
    post_forward,
    query_gain,
    key_gain,
    query_weight,
    key_weight,
    value_weight,
    output_weight,
    gate_rows,
    up_rows,
    down_rows,
):
    rows = tokens.shape[0]
    width = tokens.shape[1]
    head_size = key_weight.shape[1]
    heads = query_weight.shape[1] // head_size
    features = heads * head_size
    span = features + 2 * head_size
    devices = NZ * NH * NC
    own_rows = query_weight.shape[0]
    own_gain = query_gain.shape[0]
    chips_back = (WINDOW + NC * rows - 1) // (NC * rows)
    shard = lax.axis_index("fsdp")
    local_index = shard * rows + jnp.arange(rows, dtype=jnp.int32)
    other = shard + 1 - 2 * (shard % NC)
    key_index = jnp.concatenate(
        [
            (core - back * NC) * rows + jnp.arange(rows, dtype=jnp.int32)
            for core in (shard, other)
            for back in range(chips_back, -1, -1)
        ]
    )
    query_seg, query_pos = doc_info(lengths[0], local_index)
    key_seg, key_place = doc_info(lengths[0], key_index)
    distance = local_index[:, None] - key_index[None, :]
    allowed = (query_seg[:, None] == key_seg[None, :]) & (distance >= 0) & (distance < WINDOW)

    gains = (pre_attention, post_attention, pre_forward, post_forward, query_gain, key_gain)
    lines = [jnp.pad(g[None, :], ((0, 0), (0, span - g.shape[0]))) for g in gains]
    packed = jnp.concatenate(
        [
            jnp.concatenate([query_weight, key_weight, value_weight], axis=1),
            *lines,
            jnp.zeros((GAIN_LINES - len(lines), span), LOW),
        ],
        axis=0,
    )
    weight_out = lax.all_gather(output_weight, "fsdp", axis=0, tiled=True)
    feed_own = (gate_rows, up_rows, down_rows)
    first_all, feed_own = in_offset_order(gather_chips(packed), feed_own)
    feed_other = tuple(swap(w) for w in feed_own)
    weight_in = first_all[:, :own_rows].reshape(width, span)
    gain_all = to_mesh_order(first_all[:, own_rows:, :own_rows]).astype(F32)
    gain_pre_att, gain_post_att, gain_pre_fwd, gain_post_fwd = (
        gain_all[:, k].reshape(width) for k in range(4)
    )
    gain_query, gain_key = (gain_all[:, 4 + k, :own_gain].reshape(head_size) for k in range(2))

    inputs = tokens.astype(F32)
    normed_one, pull_one = jax.vjp(norm_rows, inputs, gain_pre_att)
    normed_low = normed_one.astype(LOW)
    normed_rel = to_relative(normed_low.T.reshape(devices, own_rows, rows)).reshape(width, rows)
    linear = dot(normed_rel, weight_in, CONTRACT_FIRST)
    query_lin = linear[:, :features]
    key_lin = linear[:, features : features + head_size]
    value_low = linear[:, features + head_size :].astype(LOW)

    table = rope_table(query_pos, head_size)
    query_heads = norm_rows(query_lin.reshape(rows, heads, head_size), gain_query)
    query_value = (rotate(query_heads, table) * head_size**-0.5).reshape(rows, features)

    def key_side(lin, gain):
        return rotate(norm_rows(lin[:, None, :], gain), table)[:, 0, :]

    key_value, pull_key = jax.vjp(key_side, key_lin, gain_key)
    query_low = query_value.astype(LOW)
    key_low = key_value.astype(LOW)
    outgoing = jnp.concatenate([key_low, value_low], axis=1)
    outgoing, feed_other = lax.optimization_barrier((outgoing, feed_other))
    feed_weights = [w for both in zip(feed_own, feed_other) for w in both]
    arrived = [shifted(outgoing, "fsdp", NC * back) for back in range(chips_back, 0, -1)]
    mine = jnp.concatenate(arrived + [outgoing], axis=0)
    both = jnp.concatenate([mine, swap(mine)], axis=0)
    mask = allowed.astype(F32)
    gain_lines = jnp.stack([gain_post_att, gain_pre_fwd])
    line, wide = ((rows, width), (rows, features))
    mixed_low, projected, residual_one, normed_two_low = whole_call(
        attend_kernel,
        [
            jax.ShapeDtypeStruct(wide, LOW),
            jax.ShapeDtypeStruct(line, F32),
            jax.ShapeDtypeStruct(line, F32),
            jax.ShapeDtypeStruct(line, LOW),
        ],
        2 * rows * features * (width + 2 * both.shape[0]),
        (query_low, both, mask, weight_out, tokens, gain_lines),
    )
    mixed_rel = to_relative(mixed_low.T.reshape(devices, -1, rows)).reshape(features, rows)
    _, pull_two = jax.vjp(norm_rows, projected, gain_post_att)
    _, pull_three = jax.vjp(norm_rows, residual_one, gain_pre_fwd)

    normed_of = gather_chips(normed_two_low)
    acts, sent = ([], [])
    for offsets in (NEAR, FAR):
        pieces = [piece for p in offsets for piece in normed_of[p]]
        *kept, down = feed(pieces, feed_weights)
        acts.append(kept)
        sent.append(handed(offsets, down))
    down_sum = sum_of(sent)
    fed, pull_four = jax.vjp(norm_rows, down_sum, gain_post_fwd)
    output = (residual_one + fed).astype(LOW)
    grad_out = cotangent.astype(F32)
    grad_down, grad_post_fwd = pull_four(grad_out)
    grad_down_of = gather_chips(grad_down.astype(LOW))
    backs, sent = ([], [])
    for offsets, kept in zip((NEAR, FAR), acts):
        pieces = [piece for p in offsets for piece in grad_down_of[p]]
        *grads, back = feed_back(pieces, feed_weights, kept[1:3], kept[3:5])
        backs.append(grads)
        sent.append(handed(offsets, back))
    backs, sent[0] = lax.optimization_barrier((backs, sent[0]))
    normed_chunks, grad_chunks = ([kept[0] for kept in acts], [grads[0] for grads in backs])
    products = [
        [
            ([grads[1 + core] for grads in backs], normed_chunks),
            ([grads[3 + core] for grads in backs], normed_chunks),
            ([kept[5 + core] for kept in acts], grad_chunks),
        ]
        for core in range(NC)
    ]
    hidden_rows = gate_rows.shape[0]
    rows_sum = row_gradients(products[0], [swap(row_gradients(products[1]))])
    sent[1][-1], rows_sum = lax.optimization_barrier((sent[1][-1], rows_sum))
    grad_normed_two = sum_of(sent)
    rows_share = y_part(rows_sum)

    extra_three, grad_pre_fwd = pull_three(grad_normed_two)
    grad_residual = grad_out + extra_three
    grad_projected, grad_post_att = pull_two(grad_residual)
    grad_proj_low = grad_projected.astype(LOW)
    half = (chips_back + 1) * rows
    query_lin_low, grad_query_gain, grad_own, grad_away = whole_call(
        attend_back_kernel,
        [
            jax.ShapeDtypeStruct(wide, LOW),
            jax.ShapeDtypeStruct((1, head_size), F32),
            jax.ShapeDtypeStruct((half, 2 * head_size), F32),
            jax.ShapeDtypeStruct((half, 2 * head_size), LOW),
        ],
        2 * rows * features * (width + 5 * both.shape[0]),
        (
            grad_proj_low,
            weight_out,
            query_low,
            both,
            mask,
            query_lin,
            jnp.concatenate(table, axis=1),
            gain_query[None, :],
        ),
        [pltpu.VMEM((2 * half, 2 * head_size), F32)],
    )
    grad_query_gain = grad_query_gain[0]
    grad_both = grad_own + swap(grad_away).astype(F32)
    grad_both, query_lin_low, grad_proj_low = lax.optimization_barrier(
        (grad_both, query_lin_low, grad_proj_low)
    )
    lines = own_rows + (features // devices) * width // features
    sums = chip_sums(
        *block_call(
            wide_kernel, lines, features, (normed_rel, query_lin_low, mixed_rel, grad_proj_low)
        )
    )
    owned_both = grad_both[chips_back * rows :]
    for back in range(1, chips_back + 1):
        piece = grad_both[(chips_back - back) * rows : (chips_back - back + 1) * rows]
        owned_both = owned_both + shifted(piece.astype(LOW), "fsdp", -NC * back).astype(F32)
    owned_both, rows_share, sums = lax.optimization_barrier((owned_both, rows_share, sums))
    wide_part = z_sums(sums)
    rows_share = x_sum(rows_share)
    grad_key_low = owned_both[:, :head_size].astype(LOW)
    grad_value_low = owned_both[:, head_size:].astype(LOW)
    grad_key_lin, grad_key_gain = pull_key(grad_key_low.astype(F32))
    pair_low = jnp.concatenate([grad_key_lin.astype(LOW), grad_value_low], axis=1)
    grad_linear = jnp.concatenate([query_lin_low, pair_low], axis=1)
    grad_normed_rel = dot(weight_in, grad_linear, CONTRACT_LAST)
    grad_normed_one = to_mesh_order(grad_normed_rel.reshape(devices, own_rows, rows))
    grad_normed_one = grad_normed_one.reshape(width, rows).T
    extra_one, grad_pre_att = pull_one(grad_normed_one)
    grad_inputs = grad_residual + extra_one
    gain_grads = jnp.stack(
        [
            jnp.pad(g.reshape(devices, -1), ((0, 0), (0, own_rows - g.shape[0] // devices)))
            for g in (
                grad_pre_att,
                grad_post_att,
                grad_pre_fwd,
                grad_post_fwd,
                grad_query_gain,
                grad_key_gain,
            )
        ],
        axis=1,
    )
    gain_grads = to_relative(gain_grads)
    gain_grads = jnp.pad(
        gain_grads,
        ((0, 0), (0, GAIN_LINES - gain_grads.shape[1]), (0, 2 * head_size - own_rows)),
    ).reshape(-1, 2 * head_size)
    pair_sums = chip_sums(
        *block_call(
            pair_kernel, own_rows + GAIN_LINES, 2 * head_size, (normed_rel, pair_low, gain_grads)
        )
    )
    pair_sums, wide_part, rows_share = lax.optimization_barrier(
        (pair_sums, wide_part, rows_share)
    )
    rows_whole = y_whole(rows_share)
    wide_part = pair_sum(wide_part)
    pair_part = pair_sum(z_sums(pair_sums))
    middle = pair_part.shape[0] // 2
    share = jnp.concatenate(
        [wide_part, jnp.concatenate([pair_part[:middle], pair_part[middle:]], axis=1)], axis=0
    )
    spare = -share.shape[0] % (16 * NY)
    share = jnp.pad(share, ((0, spare), (0, 0))).astype(LOW)
    share, rows_whole = rep_sum(share, rows_whole)
    owned_query = share[:own_rows]
    owned_output = unfolded(share[own_rows : wide_part.shape[0]], width)
    pair_lines = share[wide_part.shape[0] : wide_part.shape[0] + middle]
    owned_pair = jnp.concatenate(jnp.split(pair_lines, 2, axis=1), axis=0)
    owned_gains = [owned_pair[own_rows + k, :own_rows] for k in range(4)]
    owned_gains += [owned_pair[own_rows + 4 + k, :own_gain] for k in range(2)]
    owned_pair = owned_pair[:own_rows]
    rows_whole = rows_whole[:hidden_rows].astype(F32)
    return (
        output,
        grad_inputs,
        *owned_gains,
        owned_query,
        owned_pair[:, :head_size],
        owned_pair[:, head_size:],
        owned_output,
        rows_whole[:, :width],
        rows_whole[:, width : 2 * width],
        rows_whole[:, 2 * width :],
    )


def solution(mesh):
    tokens, weight, vector = (P(("rep", "fsdp"), None), P("fsdp", None), P("fsdp"))
    return jax.shard_map(
        local,
        mesh=mesh,
        in_specs=(tokens, P("rep", None), tokens) + (vector,) * 6 + (weight,) * 7,
        out_specs=(tokens, tokens) + (vector,) * 6 + (weight,) * 7,
        check_vma=False,
    )
```

```python
import functools
import math

import jax
import jax.numpy as jnp
from jax import lax
from jax.experimental import pallas as pl
from jax.experimental.pallas import tpu as pltpu
from jax.sharding import PartitionSpec as P

WINDOW = 512
EPSILON = 1e-06
MASKED = -1e30
CONTRACT_LAST = (((1,), (1,)), ((), ()))
CONTRACT_FIRST = (((0,), (0,)), ((), ()))
F32 = jnp.float32
LOW = jnp.bfloat16
NZ, NH, NC = (4, 2, 2)
GAIN_LINES = 8
NY, NX = (4, 2)
PEERS = [(1, 0), (3, 0), (0, 1), (1, 1), (3, 1), (2, 0), (2, 1)]
NEAR = [(0, 0), (0, 1), (1, 0), (3, 0)]
FAR = [(1, 1), (3, 1), (2, 0), (2, 1)]
TILE = 256
ROW_GRANULE = 64
VMEM = 44 * 2**20


def place(z, h, c):
    return (z % NZ * NH + h % NH) * NC + c % NC


def route(dz, dh, dc):
    return [
        (place(z + dz, h + dh, c + dc), place(z, h, c))
        for z in range(NZ)
        for h in range(NH)
        for c in range(NC)
    ]


def fetch(block, dz, dh, dc=0):
    return lax.ppermute(block, "fsdp", route(dz, dh, dc))


def hand(block, dz, dh, dc=0):
    return fetch(block, -dz, -dh, -dc)


def swap(block):
    return fetch(block, 0, 0, 1)


def gather_chips(block):
    rows = block.shape[0]
    half = rows // 2
    pair = fetch(block, 0, 1)
    up, down = (fetch(block, 1, 0), fetch(block, 3, 0))
    above = fetch(jnp.concatenate([pair, up[:half]], axis=0), 1, 0)
    below = fetch(jnp.concatenate([pair, down[half:]], axis=0), 3, 0)
    last = (fetch(above[:half], 1, 0), fetch(below[half:rows], 3, 0))
    return {
        (0, 0): [block],
        (0, 1): [pair],
        (1, 0): [up],
        (3, 0): [down],
        (1, 1): [above[:rows]],
        (3, 1): [below[:rows]],
        (2, 0): [above[rows:], below[rows:]],
        (2, 1): list(last),
    }


def coordinates():
    me = lax.axis_index("fsdp")
    return (me // (NH * NC), me // NC % NH, me % NC)


def turned(blocks, start):
    twice = jnp.concatenate([blocks, blocks], axis=0)
    return lax.dynamic_slice_in_dim(twice, start, NZ, 0)


def flipped(blocks, amount, axis):
    return jnp.where(amount == 0, blocks, jnp.flip(blocks, axis))


def to_relative(lines):
    z, h, c = coordinates()
    blocks = lines.reshape(NZ, NH, NC, -1, *lines.shape[1:])
    return flipped(flipped(turned(blocks, z), h, 1), c, 2).reshape(lines.shape)


def to_mesh_order(lines):
    z, h, c = coordinates()
    blocks = lines.reshape(NZ, NH, NC, -1, *lines.shape[1:])
    return flipped(flipped(turned(blocks, (NZ - z) % NZ), h, 1), c, 2).reshape(lines.shape)


def in_offset_order(chips, after):
    mine = jnp.stack(
        [jnp.concatenate(chips[z, h], axis=0) for z in range(NZ) for h in range(NH)]
    )
    mine, after = lax.optimization_barrier((mine, after))
    other = swap(mine)
    both = jnp.stack([mine, other], axis=1)
    return both.reshape(NZ * NH * NC, *mine.shape[1:]), after


def handed(offsets, values):
    rows = values.shape[0] // len(offsets)
    arrived = []
    for k, p in enumerate(offsets):
        block = values[k * rows : (k + 1) * rows]
        arrived.append(block if p == (0, 0) else hand(block, *p))
    return arrived


def sum_of(lists):
    total = None
    for arrived in lists:
        for block in arrived:
            total = block.astype(F32) if total is None else total + block.astype(F32)
    return total


def unfolded(lines, width):
    columns = lines.shape[1]
    count = lines.shape[0] * columns // width
    rest = jnp.split(lines[count:], columns // (width - columns), axis=1)
    return jnp.concatenate([lines[:count], jnp.concatenate(rest, axis=0)], axis=1)


def chip_sums(mine, away):
    total = (mine.astype(F32) + swap(away).astype(F32)).astype(LOW)
    return total.reshape(NZ, NH, -1, mine.shape[1])


def z_sums(low):
    total = low[0].astype(F32)
    for z in (1, 3, 2):
        total = total + hand(low[z], z, 0).astype(F32)
    return total


def pair_sum(total):
    return total[0] + hand(total[1].astype(LOW), 0, 1).astype(F32)


def rep_fetch(block, dy, dx=0):
    size = lax.axis_size("rep")
    pairs = [
        ((y + dy) % (size // NX) * NX + (x + dx) % NX, y * NX + x)
        for y in range(size // NX)
        for x in range(NX)
    ]
    return lax.ppermute(block, "rep", pairs)


def lines_of(x, dy):
    number = lax.axis_size("rep") // NX
    size = x.shape[0] // number
    at = (lax.axis_index("rep") // NX + dy) % number * size
    return lax.dynamic_slice_in_dim(x, at, size, 0)


def y_part(x):
    half = x.shape[0] // (2 * NY)
    far = lines_of(x, 2)
    below = rep_fetch(far[:half], -1)
    above = rep_fetch(far[half:], 1)
    up, down = (lines_of(x, 1), lines_of(x, 3))
    up_first = (up[:half].astype(F32) + below.astype(F32)).astype(LOW)
    down_last = (down[half:].astype(F32) + above.astype(F32)).astype(LOW)
    low = rep_fetch(jnp.concatenate([up_first, up[half:]], axis=0), -1)
    high = rep_fetch(jnp.concatenate([down[:half], down_last], axis=0), 1)
    return lines_of(x, 0).astype(F32) + low.astype(F32) + high.astype(F32)


def x_sum(x):
    low = x.astype(LOW)
    return (low.astype(F32) + rep_fetch(low, 0, 1).astype(F32)).astype(LOW)


def placed(pieces):
    size = sum(values.shape[0] for dy, at, values in pieces) // NY
    whole = jnp.zeros((size * NY, pieces[0][2].shape[1]), LOW)
    y = lax.axis_index("rep") // NX
    for dy, at, values in pieces:
        whole = lax.dynamic_update_slice(whole, values, ((y + dy) % NY * size + at, 0))
    return whole


def y_near(part):
    return rep_fetch(part, 1), rep_fetch(part, -1)


def y_whole(part, up, down):
    half = part.shape[0] // 2
    first, last = (rep_fetch(up[:half], 1), rep_fetch(down[half:], -1))
    return placed([(0, 0, part), (1, 0, up), (3, 0, down), (2, 0, first), (2, half, last)])


def rep_sum(x, after):
    arrived = [rep_fetch(lines_of(x, -dy), dy) for dy in (1, 3, 2)]
    part = lines_of(x, 0).astype(F32)
    for block in arrived:
        part = part + block.astype(F32)
    part, after = lax.optimization_barrier((x_sum(part), after))
    total = placed([(0, 0, part)] + [(dy, 0, rep_fetch(part, dy)) for dy in (1, 3, 2)])
    return total.astype(F32), after


def shifted(block, axis, distance):
    devices = range(lax.axis_size(axis))
    pairs = [(i - distance, i) for i in devices if i - distance in devices]
    return lax.ppermute(block, axis, pairs)


def norm_rows(values, gain):
    return values * lax.rsqrt(jnp.mean(values * values, axis=-1, keepdims=True) + EPSILON) * gain


def rope_table(position, size):
    half = size // 2
    freq = 10000.0 ** (-2.0 * jnp.arange(half, dtype=F32) / size)
    angle = position.astype(F32)[:, None] * freq[None, :]
    return jnp.cos(angle), jnp.sin(angle)


def rotate(values, table):
    half = values.shape[-1] // 2
    cosine, sine = (part[:, None, :] for part in table)
    first = values[..., :half]
    second = values[..., half:]
    return jnp.concatenate(
        [first * cosine - second * sine, second * cosine + first * sine], axis=-1
    )


def doc_info(lengths, index):
    ends = jnp.cumsum(lengths)
    starts = ends - lengths
    segment = jnp.sum((index[:, None] >= ends[None, :-1]).astype(jnp.int32), axis=1)
    hit = segment[:, None] == jnp.arange(lengths.shape[0], dtype=jnp.int32)[None, :]
    first = jnp.sum(jnp.where(hit, starts[None, :], 0), axis=1)
    segment = jnp.where(index < 0, -1, segment)
    return (segment, index - first)


def dot(a, b, dims=(((1,), (0,)), ((), ()))):
    return lax.dot_general(a, b, dims, preferred_element_type=F32)


GELU_SCALE = math.sqrt(2.0 / math.pi)
GELU_CUBE = 0.044715


def join(pieces, whole):
    at = 0
    for piece in pieces:
        whole[at : at + piece.shape[0], :] = piece[...]
        at += piece.shape[0]


def feed_kernel(count, *refs):
    pieces, weights, (x, *saved, out) = (refs[:count], refs[count : count + 6], refs[count + 6 :])
    join(pieces, x)

    @pl.loop(0, x.shape[0] // TILE)
    def _(step):
        lines = pl.ds(pl.multiple_of(step * TILE, TILE), TILE)
        block = x[lines, :]
        total = None
        for half in range(2):
            gate_w, up_w, down_w = weights[half::2]
            gate_s, up_s, hidden_s = saved[half::2]
            gate = dot(block, gate_w[...], CONTRACT_LAST)
            upward = dot(block, up_w[...], CONTRACT_LAST)
            bend = jnp.tanh(GELU_SCALE * (gate + GELU_CUBE * gate * gate * gate))
            hidden = (0.5 * gate * (1.0 + bend) * upward).astype(LOW)
            gate_s[lines, :] = gate.astype(LOW)
            up_s[lines, :] = upward.astype(LOW)
            hidden_s[lines, :] = hidden
            part = dot(hidden, down_w[...])
            total = part if total is None else total + part
        out[lines, :] = total.astype(LOW)


def back_kernel(count, *refs):
    pieces, weights = (refs[:count], refs[count : count + 6])
    gates, ups = (refs[count + 6 : count + 8], refs[count + 8 : count + 10])
    grad, *saved, out = refs[count + 10 :]
    join(pieces, grad)

    @pl.loop(0, grad.shape[0] // TILE)
    def _(step):
        lines = pl.ds(pl.multiple_of(step * TILE, TILE), TILE)
        block = grad[lines, :]
        total = None
        for half in range(2):
            gate_w, up_w, down_w = weights[half::2]
            grad_hidden = dot(block, down_w[...], CONTRACT_LAST)
            gate = gates[half][lines, :].astype(F32)
            upward = ups[half][lines, :].astype(F32)
            square = gate * gate
            bend = jnp.tanh(GELU_SCALE * gate * (1.0 + GELU_CUBE * square))
            rise = 0.5 * (1.0 + bend)
            slope = rise + 0.5 * gate * (1.0 - bend * bend) * (
                GELU_SCALE * (1.0 + 3.0 * GELU_CUBE * square)
            )
            grad_gate = (grad_hidden * upward * slope).astype(LOW)
            grad_up = (grad_hidden * gate * rise).astype(LOW)
            saved[half][lines, :] = grad_gate
            saved[2 + half][lines, :] = grad_up
            part = dot(grad_gate, gate_w[...]) + dot(grad_up, up_w[...])
            total = part if total is None else total + part
        out[lines, :] = total.astype(LOW)


def rows_kernel(count, *refs):
    out = refs[-1]
    hidden, width = (refs[0].shape[1], refs[2].shape[1])
    for k in range(count):
        left, right = (refs[4 * k : 4 * k + 2], refs[4 * k + 2 : 4 * k + 4])
        columns = slice(k * width, (k + 1) * width)
        total = dot(left[0][...], right[0][...], CONTRACT_FIRST)
        total = total + dot(left[1][...], right[1][...], CONTRACT_FIRST)
        if len(refs) > 4 * count + 1:
            total = total + refs[4 * count][:hidden, columns].astype(F32)
        out[:hidden, columns] = total.astype(LOW)
    out[hidden:, :] = jnp.zeros((out.shape[0] - hidden, out.shape[1]), LOW)


def head_slices(queries, head_size):
    return [slice(at, at + head_size) for at in range(0, queries.shape[1], head_size)]


def masked_softmax(query, keys, mask):
    scores = jnp.where(mask > 0, dot(query, keys, CONTRACT_LAST), MASKED)
    expo = jnp.exp(scores - jnp.max(scores, axis=-1, keepdims=True))
    return expo / jnp.sum(expo, axis=-1, keepdims=True)


def attend_kernel(query, both, mask, weight, inputs, gains, mixed, projected, residual, normed):
    size = both.shape[1] // 2
    keys, values, allowed = (both[:, :size], both[:, size:], mask[...])
    for columns in head_slices(query, size):
        probs = masked_softmax(query[:, columns], keys, allowed)
        mixed[:, columns] = dot(probs.astype(LOW), values).astype(LOW)
    lines = dot(mixed[...], weight[...])
    projected[...] = lines
    lines = inputs[...].astype(F32) + norm_rows(lines, gains[0:1, :])
    residual[...] = lines
    normed[...] = norm_rows(lines, gains[1:2, :]).astype(LOW)


def attend_back_kernel(
    grad, weight, query, both, mask, linear, turns, gain, out, grad_gain, own, away, total
):
    size = both.shape[1] // 2
    half = size // 2
    keys, values, allowed = (both[:, :size], both[:, size:], mask[...])
    cosine, sine = (turns[:, :half], turns[:, half:])
    grad_gain[...] = jnp.zeros_like(grad_gain)
    for head, columns in enumerate(head_slices(query, size)):
        probs = masked_softmax(query[:, columns], keys, allowed)
        grad_mixed = dot(grad[...], weight[columns, :], CONTRACT_LAST).astype(LOW)
        grad_probs = dot(grad_mixed, values, CONTRACT_LAST)
        inner = jnp.sum(grad_probs * probs, axis=-1, keepdims=True)
        grad_scores = (probs * (grad_probs - inner)).astype(LOW)
        grad_keys = dot(grad_scores, query[:, columns], CONTRACT_FIRST)
        grad_values = dot(probs.astype(LOW), grad_mixed, CONTRACT_FIRST)
        if head == 0:
            total[:, :size] = grad_keys
            total[:, size:] = grad_values
        else:
            total[:, :size] += grad_keys
            total[:, size:] += grad_values
        turned_grad = dot(grad_scores, keys).astype(LOW).astype(F32) * size**-0.5
        first, second = (turned_grad[:, :half], turned_grad[:, half:])
        grad_normed = jnp.concatenate(
            [first * cosine + second * sine, second * cosine - first * sine], axis=1
        )
        lines = linear[:, columns]
        scale = lax.rsqrt(jnp.mean(lines * lines, axis=-1, keepdims=True) + EPSILON)
        grad_gain[0:1, :] += jnp.sum(grad_normed * lines * scale, axis=0, keepdims=True)
        grad_normed = grad_normed * gain[0:1, :]
        share = jnp.mean(grad_normed * lines, axis=-1, keepdims=True)
        out[:, columns] = (scale * grad_normed - lines * (scale * scale * scale * share)).astype(LOW)
    kept = own.shape[0]
    own[...] = total[:kept, :]
    away[...] = total[kept:, :].astype(LOW)


def wide_kernel(inputs, query, mixed, grad, mine, away, block):
    devices, columns = (mine.shape[0] * 2 // block.shape[0], query.shape[1])
    query_grad = dot(inputs[...], query[...])
    output_grad = dot(mixed[...], grad[...])
    own, lines = (query_grad.shape[0] // devices, output_grad.shape[0] // devices)
    rest = output_grad.shape[1] - columns
    size = lines * rest // columns
    for number in range(devices):
        part = output_grad[number * lines : (number + 1) * lines]
        block[:own, :] = query_grad[number * own : (number + 1) * own]
        block[own : own + lines, :] = part[:, :columns]
        for k in range(columns // rest):
            block[own + lines :, k * rest : (k + 1) * rest] = part[
                k * size : (k + 1) * size, columns:
            ]
        out = away if number % 2 else mine
        at = number // 2 * block.shape[0]
        out[at : at + block.shape[0], :] = block[...].astype(LOW)


def pair_kernel(inputs, pair, gains, mine, away, block):
    pair_grad = dot(inputs[...], pair[...])
    devices = mine.shape[0] * 2 // block.shape[0]
    own = pair_grad.shape[0] // devices
    more = block.shape[0] - own
    for number in range(devices):
        block[:own, :] = pair_grad[number * own : (number + 1) * own]
        block[own:, :] = gains[number * more : (number + 1) * more, :]
        out = away if number % 2 else mine
        at = number // 2 * block.shape[0]
        out[at : at + block.shape[0], :] = block[...].astype(LOW)


def block_call(kernel, lines, columns, args):
    half = jax.ShapeDtypeStruct((NZ * NH * lines, columns), LOW)
    flops = 4 * args[0].shape[0] * args[0].shape[1] * columns
    return whole_call(kernel, [half, half], flops, args, [pltpu.VMEM((lines, columns), F32)])


def whole_call(kernel, shapes, flops, args, scratch=()):
    moved = sum(math.prod(a.shape) * 2 for a in (*args, *shapes))
    return pl.pallas_call(
        kernel,
        out_shape=shapes,
        in_specs=[pl.BlockSpec(memory_space=pltpu.VMEM)] * len(args),
        out_specs=[pl.BlockSpec(memory_space=pltpu.VMEM)] * len(shapes),
        scratch_shapes=scratch,
        compiler_params=pltpu.CompilerParams(vmem_limit_bytes=VMEM),
        cost_estimate=pl.CostEstimate(flops=flops, bytes_accessed=moved, transcendentals=0),
    )(*args)


def feed(pieces, weights):
    rows, (hidden, width) = (sum(p.shape[0] for p in pieces), weights[0].shape)
    shapes = [jax.ShapeDtypeStruct((rows, n), LOW) for n in [width] + [hidden] * 6 + [width]]
    return whole_call(
        functools.partial(feed_kernel, len(pieces)),
        shapes,
        12 * rows * hidden * width,
        (*pieces, *weights),
    )


def feed_back(pieces, weights, gates, ups):
    rows, (hidden, width) = (sum(p.shape[0] for p in pieces), weights[0].shape)
    shapes = [jax.ShapeDtypeStruct((rows, n), LOW) for n in [width] + [hidden] * 4 + [width]]
    return whole_call(
        functools.partial(back_kernel, len(pieces)),
        shapes,
        12 * rows * hidden * width,
        (*pieces, *weights, *gates, *ups),
    )


def row_gradients(pairs, added=()):
    args = [a for left, right in pairs for a in (*left, *right)]
    rows, hidden = args[0].shape
    width = args[2].shape[1]
    lines = hidden + -hidden % ROW_GRANULE
    return whole_call(
        functools.partial(rows_kernel, len(pairs)),
        [jax.ShapeDtypeStruct((lines, len(pairs) * width), LOW)],
        4 * len(pairs) * rows * hidden * width,
        (*args, *added),
    )[0]


def local(
    tokens,
    lengths,
    cotangent,
    pre_attention,
    post_attention,
    pre_forward,
    post_forward,
    query_gain,
    key_gain,
    query_weight,
    key_weight,
    value_weight,
    output_weight,
    gate_rows,
    up_rows,
    down_rows,
):
    rows = tokens.shape[0]
    width = tokens.shape[1]
    head_size = key_weight.shape[1]
    heads = query_weight.shape[1] // head_size
    features = heads * head_size
    span = features + 2 * head_size
    devices = NZ * NH * NC
    own_rows = query_weight.shape[0]
    own_gain = query_gain.shape[0]
    chips_back = (WINDOW + NC * rows - 1) // (NC * rows)
    shard = lax.axis_index("fsdp")
    local_index = shard * rows + jnp.arange(rows, dtype=jnp.int32)
    other = shard + 1 - 2 * (shard % NC)
    key_index = jnp.concatenate(
        [
            (core - back * NC) * rows + jnp.arange(rows, dtype=jnp.int32)
            for core in (shard, other)
            for back in range(chips_back, -1, -1)
        ]
    )
    query_seg, query_pos = doc_info(lengths[0], local_index)
    key_seg, key_place = doc_info(lengths[0], key_index)
    distance = local_index[:, None] - key_index[None, :]
    allowed = (query_seg[:, None] == key_seg[None, :]) & (distance >= 0) & (distance < WINDOW)

    gains = (pre_attention, post_attention, pre_forward, post_forward, query_gain, key_gain)
    lines = [jnp.pad(g[None, :], ((0, 0), (0, span - g.shape[0]))) for g in gains]
    packed = jnp.concatenate(
        [
            jnp.concatenate([query_weight, key_weight, value_weight], axis=1),
            *lines,
            jnp.zeros((GAIN_LINES - len(lines), span), LOW),
        ],
        axis=0,
    )
    weight_out = lax.all_gather(output_weight, "fsdp", axis=0, tiled=True)
    feed_own = (gate_rows, up_rows, down_rows)
    first_all, feed_own = in_offset_order(gather_chips(packed), feed_own)
    feed_other = tuple(swap(w) for w in feed_own)
    weight_in = first_all[:, :own_rows].reshape(width, span)
    gain_all = to_mesh_order(first_all[:, own_rows:, :own_rows]).astype(F32)
    gain_pre_att, gain_post_att, gain_pre_fwd, gain_post_fwd = (
        gain_all[:, k].reshape(width) for k in range(4)
    )
    gain_query, gain_key = (gain_all[:, 4 + k, :own_gain].reshape(head_size) for k in range(2))

    inputs = tokens.astype(F32)
    normed_one, pull_one = jax.vjp(norm_rows, inputs, gain_pre_att)
    normed_low = normed_one.astype(LOW)
    normed_rel = to_relative(normed_low.T.reshape(devices, own_rows, rows)).reshape(width, rows)
    linear = dot(normed_rel, weight_in, CONTRACT_FIRST)
    query_lin = linear[:, :features]
    key_lin = linear[:, features : features + head_size]
    value_low = linear[:, features + head_size :].astype(LOW)

    table = rope_table(query_pos, head_size)
    query_heads = norm_rows(query_lin.reshape(rows, heads, head_size), gain_query)
    query_value = (rotate(query_heads, table) * head_size**-0.5).reshape(rows, features)

    def key_side(lin, gain):
        return rotate(norm_rows(lin[:, None, :], gain), table)[:, 0, :]

    key_value, pull_key = jax.vjp(key_side, key_lin, gain_key)
    query_low = query_value.astype(LOW)
    key_low = key_value.astype(LOW)
    outgoing = jnp.concatenate([key_low, value_low], axis=1)
    outgoing, feed_other = lax.optimization_barrier((outgoing, feed_other))
    feed_weights = [w for both in zip(feed_own, feed_other) for w in both]
    arrived = [shifted(outgoing, "fsdp", NC * back) for back in range(chips_back, 0, -1)]
    mine = jnp.concatenate(arrived + [outgoing], axis=0)
    both = jnp.concatenate([mine, swap(mine)], axis=0)
    mask = allowed.astype(F32)
    gain_lines = jnp.stack([gain_post_att, gain_pre_fwd])
    line, wide = ((rows, width), (rows, features))
    mixed_low, projected, residual_one, normed_two_low = whole_call(
        attend_kernel,
        [
            jax.ShapeDtypeStruct(wide, LOW),
            jax.ShapeDtypeStruct(line, F32),
            jax.ShapeDtypeStruct(line, F32),
            jax.ShapeDtypeStruct(line, LOW),
        ],
        2 * rows * features * (width + 2 * both.shape[0]),
        (query_low, both, mask, weight_out, tokens, gain_lines),
    )
    mixed_rel = to_relative(mixed_low.T.reshape(devices, -1, rows)).reshape(features, rows)
    _, pull_two = jax.vjp(norm_rows, projected, gain_post_att)
    _, pull_three = jax.vjp(norm_rows, residual_one, gain_pre_fwd)

    normed_of = gather_chips(normed_two_low)
    acts, sent = ([], [])
    for offsets in (NEAR, FAR):
        pieces = [piece for p in offsets for piece in normed_of[p]]
        *kept, down = feed(pieces, feed_weights)
        acts.append(kept)
        sent.append(handed(offsets, down))
    down_sum = sum_of(sent)
    fed, pull_four = jax.vjp(norm_rows, down_sum, gain_post_fwd)
    output = (residual_one + fed).astype(LOW)
    grad_out = cotangent.astype(F32)
    grad_down, grad_post_fwd = pull_four(grad_out)
    grad_down_of = gather_chips(grad_down.astype(LOW))
    backs, sent = ([], [])
    for offsets, kept in zip((NEAR, FAR), acts):
        pieces = [piece for p in offsets for piece in grad_down_of[p]]
        *grads, back = feed_back(pieces, feed_weights, kept[1:3], kept[3:5])
        backs.append(grads)
        sent.append(handed(offsets, back))
    backs, sent[0] = lax.optimization_barrier((backs, sent[0]))
    normed_chunks, grad_chunks = ([kept[0] for kept in acts], [grads[0] for grads in backs])
    products = [
        [
            ([grads[1 + core] for grads in backs], normed_chunks),
            ([grads[3 + core] for grads in backs], normed_chunks),
            ([kept[5 + core] for kept in acts], grad_chunks),
        ]
        for core in range(NC)
    ]
    hidden_rows = gate_rows.shape[0]
    rows_sum = row_gradients(products[0]).astype(F32)
    rows_sum = (rows_sum + swap(row_gradients(products[1])).astype(F32)).astype(LOW)
    sent[1][-1], rows_sum = lax.optimization_barrier((sent[1][-1], rows_sum))
    grad_normed_two = sum_of(sent)
    rows_share = y_part(rows_sum)

    extra_three, grad_pre_fwd = pull_three(grad_normed_two)
    grad_residual = grad_out + extra_three
    grad_projected, grad_post_att = pull_two(grad_residual)
    grad_proj_low = grad_projected.astype(LOW)
    half = (chips_back + 1) * rows
    query_lin_low, grad_query_gain, grad_own, grad_away = whole_call(
        attend_back_kernel,
        [
            jax.ShapeDtypeStruct(wide, LOW),
            jax.ShapeDtypeStruct((1, head_size), F32),
            jax.ShapeDtypeStruct((half, 2 * head_size), F32),
            jax.ShapeDtypeStruct((half, 2 * head_size), LOW),
        ],
        2 * rows * features * (width + 5 * both.shape[0]),
        (
            grad_proj_low,
            weight_out,
            query_low,
            both,
            mask,
            query_lin,
            jnp.concatenate(table, axis=1),
            gain_query[None, :],
        ),
        [pltpu.VMEM((2 * half, 2 * head_size), F32)],
    )
    grad_query_gain = grad_query_gain[0]
    grad_both = grad_own + swap(grad_away).astype(F32)
    grad_both, query_lin_low, grad_proj_low = lax.optimization_barrier(
        (grad_both, query_lin_low, grad_proj_low)
    )
    lines = own_rows + (features // devices) * width // features
    sums = chip_sums(
        *block_call(
            wide_kernel, lines, features, (normed_rel, query_lin_low, mixed_rel, grad_proj_low)
        )
    )
    owned_both = grad_both[chips_back * rows :]
    for back in range(1, chips_back + 1):
        piece = grad_both[(chips_back - back) * rows : (chips_back - back + 1) * rows]
        owned_both = owned_both + shifted(piece.astype(LOW), "fsdp", -NC * back).astype(F32)
    owned_both, sums = lax.optimization_barrier((owned_both, sums))
    rows_share, _ = lax.optimization_barrier((rows_share, sums))
    wide_part = z_sums(sums)
    rows_share = x_sum(rows_share)
    grad_key_low = owned_both[:, :head_size].astype(LOW)
    grad_value_low = owned_both[:, head_size:].astype(LOW)
    grad_key_lin, grad_key_gain = pull_key(grad_key_low.astype(F32))
    pair_low = jnp.concatenate([grad_key_lin.astype(LOW), grad_value_low], axis=1)
    grad_linear = jnp.concatenate([query_lin_low, pair_low], axis=1)
    grad_normed_rel = dot(weight_in, grad_linear, CONTRACT_LAST)
    grad_normed_one = to_mesh_order(grad_normed_rel.reshape(devices, own_rows, rows))
    grad_normed_one = grad_normed_one.reshape(width, rows).T
    extra_one, grad_pre_att = pull_one(grad_normed_one)
    grad_inputs = grad_residual + extra_one
    gain_grads = jnp.stack(
        [
            jnp.pad(g.reshape(devices, -1), ((0, 0), (0, own_rows - g.shape[0] // devices)))
            for g in (
                grad_pre_att,
                grad_post_att,
                grad_pre_fwd,
                grad_post_fwd,
                grad_query_gain,
                grad_key_gain,
            )
        ],
        axis=1,
    )
    gain_grads = to_relative(gain_grads)
    gain_grads = jnp.pad(
        gain_grads,
        ((0, 0), (0, GAIN_LINES - gain_grads.shape[1]), (0, 2 * head_size - own_rows)),
    ).reshape(-1, 2 * head_size)
    pair_sums = chip_sums(
        *block_call(
            pair_kernel, own_rows + GAIN_LINES, 2 * head_size, (normed_rel, pair_low, gain_grads)
        )
    )
    pair_sums, wide_part, rows_share = lax.optimization_barrier(
        (pair_sums, wide_part, rows_share)
    )
    rows_near = y_near(rows_share)
    wide_part = pair_sum(wide_part)
    pair_part, rows_near = lax.optimization_barrier((z_sums(pair_sums), rows_near))
    rows_whole = y_whole(rows_share, *rows_near)
    pair_part = pair_sum(pair_part)
    middle = pair_part.shape[0] // 2
    share = jnp.concatenate(
        [wide_part, jnp.concatenate([pair_part[:middle], pair_part[middle:]], axis=1)], axis=0
    )
    spare = -share.shape[0] % (16 * NY)
    share = jnp.pad(share, ((0, spare), (0, 0))).astype(LOW)
    share, rows_whole = rep_sum(share, rows_whole)
    owned_query = share[:own_rows]
    owned_output = unfolded(share[own_rows : wide_part.shape[0]], width)
    pair_lines = share[wide_part.shape[0] : wide_part.shape[0] + middle]
    owned_pair = jnp.concatenate(jnp.split(pair_lines, 2, axis=1), axis=0)
    owned_gains = [owned_pair[own_rows + k, :own_rows] for k in range(4)]
    owned_gains += [owned_pair[own_rows + 4 + k, :own_gain] for k in range(2)]
    owned_pair = owned_pair[:own_rows]
    rows_whole = rows_whole[:hidden_rows].astype(F32)
    return (
        output,
        grad_inputs,
        *owned_gains,
        owned_query,
        owned_pair[:, :head_size],
        owned_pair[:, head_size:],
        owned_output,
        rows_whole[:, :width],
        rows_whole[:, width : 2 * width],
        rows_whole[:, 2 * width :],
    )


def solution(mesh):
    tokens, weight, vector = (P(("rep", "fsdp"), None), P("fsdp", None), P("fsdp"))
    return jax.shard_map(
        local,
        mesh=mesh,
        in_specs=(tokens, P("rep", None), tokens) + (vector,) * 6 + (weight,) * 7,
        out_specs=(tokens, tokens) + (vector,) * 6 + (weight,) * 7,
        check_vma=False,
    )
```

```python
import functools
import math

import jax
import jax.numpy as jnp
from jax import lax
from jax.experimental import pallas as pl
from jax.experimental.pallas import tpu as pltpu
from jax.sharding import PartitionSpec as P

WINDOW = 512
EPSILON = 1e-06
MASKED = -1e30
CONTRACT_LAST = (((1,), (1,)), ((), ()))
CONTRACT_FIRST = (((0,), (0,)), ((), ()))
F32 = jnp.float32
LOW = jnp.bfloat16
NZ, NH, NC = (4, 2, 2)
GAIN_LINES = 8
NY, NX = (4, 2)
PEERS = [(1, 0), (3, 0), (0, 1), (1, 1), (3, 1), (2, 0), (2, 1)]
NEAR = [(0, 0), (0, 1), (1, 0), (3, 0)]
FAR = [(1, 1), (3, 1), (2, 0), (2, 1)]
TILE = 256
ROW_GRANULE = 64
VMEM = 44 * 2**20


def place(z, h, c):
    return (z % NZ * NH + h % NH) * NC + c % NC


def route(dz, dh, dc):
    return [
        (place(z + dz, h + dh, c + dc), place(z, h, c))
        for z in range(NZ)
        for h in range(NH)
        for c in range(NC)
    ]


def fetch(block, dz, dh, dc=0):
    return lax.ppermute(block, "fsdp", route(dz, dh, dc))


def hand(block, dz, dh, dc=0):
    return fetch(block, -dz, -dh, -dc)


def swap(block):
    return fetch(block, 0, 0, 1)


def gather_chips(block):
    rows = block.shape[0]
    half = rows // 2
    pair = fetch(block, 0, 1)
    up, down = (fetch(block, 1, 0), fetch(block, 3, 0))
    above = fetch(jnp.concatenate([pair, up[:half]], axis=0), 1, 0)
    below = fetch(jnp.concatenate([pair, down[half:]], axis=0), 3, 0)
    last = (fetch(above[:half], 1, 0), fetch(below[half:rows], 3, 0))
    return {
        (0, 0): [block],
        (0, 1): [pair],
        (1, 0): [up],
        (3, 0): [down],
        (1, 1): [above[:rows]],
        (3, 1): [below[:rows]],
        (2, 0): [above[rows:], below[rows:]],
        (2, 1): list(last),
    }


def coordinates():
    me = lax.axis_index("fsdp")
    return (me // (NH * NC), me // NC % NH, me % NC)


def turned(blocks, start):
    twice = jnp.concatenate([blocks, blocks], axis=0)
    return lax.dynamic_slice_in_dim(twice, start, NZ, 0)


def flipped(blocks, amount, axis):
    return jnp.where(amount == 0, blocks, jnp.flip(blocks, axis))


def to_relative(lines):
    z, h, c = coordinates()
    blocks = lines.reshape(NZ, NH, NC, -1, *lines.shape[1:])
    return flipped(flipped(turned(blocks, z), h, 1), c, 2).reshape(lines.shape)


def to_mesh_order(lines):
    z, h, c = coordinates()
    blocks = lines.reshape(NZ, NH, NC, -1, *lines.shape[1:])
    return flipped(flipped(turned(blocks, (NZ - z) % NZ), h, 1), c, 2).reshape(lines.shape)


def in_offset_order(chips, after):
    mine = jnp.stack(
        [jnp.concatenate(chips[z, h], axis=0) for z in range(NZ) for h in range(NH)]
    )
    mine, after = lax.optimization_barrier((mine, after))
    other = swap(mine)
    both = jnp.stack([mine, other], axis=1)
    return both.reshape(NZ * NH * NC, *mine.shape[1:]), after


def handed(offsets, values):
    rows = values.shape[0] // len(offsets)
    arrived = []
    for k, p in enumerate(offsets):
        block = values[k * rows : (k + 1) * rows]
        arrived.append(block if p == (0, 0) else hand(block, *p))
    return arrived


def sum_of(lists):
    total = None
    for arrived in lists:
        for block in arrived:
            total = block.astype(F32) if total is None else total + block.astype(F32)
    return total


def unfolded(lines, width):
    columns = lines.shape[1]
    count = lines.shape[0] * columns // width
    rest = jnp.split(lines[count:], columns // (width - columns), axis=1)
    return jnp.concatenate([lines[:count], jnp.concatenate(rest, axis=0)], axis=1)


def chip_sums(mine, away):
    total = (mine.astype(F32) + swap(away).astype(F32)).astype(LOW)
    return total.reshape(NZ, NH, -1, mine.shape[1])


def z_sums(low):
    total = low[0].astype(F32)
    for z in (1, 3, 2):
        total = total + hand(low[z], z, 0).astype(F32)
    return total


def pair_sum(total):
    return total[0] + hand(total[1].astype(LOW), 0, 1).astype(F32)


def rep_fetch(block, dy, dx=0):
    size = lax.axis_size("rep")
    pairs = [
        ((y + dy) % (size // NX) * NX + (x + dx) % NX, y * NX + x)
        for y in range(size // NX)
        for x in range(NX)
    ]
    return lax.ppermute(block, "rep", pairs)


def lines_of(x, dy):
    number = lax.axis_size("rep") // NX
    size = x.shape[0] // number
    at = (lax.axis_index("rep") // NX + dy) % number * size
    return lax.dynamic_slice_in_dim(x, at, size, 0)


def y_part(x):
    half = x.shape[0] // (2 * NY)
    far = lines_of(x, 2)
    below = rep_fetch(far[:half], -1)
    above = rep_fetch(far[half:], 1)
    up, down = (lines_of(x, 1), lines_of(x, 3))
    up_first = (up[:half].astype(F32) + below.astype(F32)).astype(LOW)
    down_last = (down[half:].astype(F32) + above.astype(F32)).astype(LOW)
    low = rep_fetch(jnp.concatenate([up_first, up[half:]], axis=0), -1)
    high = rep_fetch(jnp.concatenate([down[:half], down_last], axis=0), 1)
    return lines_of(x, 0).astype(F32) + low.astype(F32) + high.astype(F32)


def x_sum(x):
    low = x.astype(LOW)
    return (low.astype(F32) + rep_fetch(low, 0, 1).astype(F32)).astype(LOW)


def placed(pieces):
    size = sum(values.shape[0] for dy, at, values in pieces) // NY
    whole = jnp.zeros((size * NY, pieces[0][2].shape[1]), LOW)
    y = lax.axis_index("rep") // NX
    for dy, at, values in pieces:
        whole = lax.dynamic_update_slice(whole, values, ((y + dy) % NY * size + at, 0))
    return whole


def y_near(part):
    return rep_fetch(part, 1), rep_fetch(part, -1)


def y_whole(part, up, down):
    half = part.shape[0] // 2
    first, last = (rep_fetch(up[:half], 1), rep_fetch(down[half:], -1))
    return placed([(0, 0, part), (1, 0, up), (3, 0, down), (2, 0, first), (2, half, last)])


def rep_sum(x, after):
    arrived = [rep_fetch(lines_of(x, -dy), dy) for dy in (1, 3, 2)]
    part = lines_of(x, 0).astype(F32)
    for block in arrived:
        part = part + block.astype(F32)
    part, after = lax.optimization_barrier((x_sum(part), after))
    total = placed([(0, 0, part)] + [(dy, 0, rep_fetch(part, dy)) for dy in (1, 3, 2)])
    return total.astype(F32), after


def shifted(block, axis, distance):
    devices = range(lax.axis_size(axis))
    pairs = [(i - distance, i) for i in devices if i - distance in devices]
    return lax.ppermute(block, axis, pairs)


def norm_rows(values, gain):
    return values * lax.rsqrt(jnp.mean(values * values, axis=-1, keepdims=True) + EPSILON) * gain


def rope_table(position, size):
    half = size // 2
    freq = 10000.0 ** (-2.0 * jnp.arange(half, dtype=F32) / size)
    angle = position.astype(F32)[:, None] * freq[None, :]
    return jnp.cos(angle), jnp.sin(angle)


def rotate(values, table):
    half = values.shape[-1] // 2
    cosine, sine = (part[:, None, :] for part in table)
    first = values[..., :half]
    second = values[..., half:]
    return jnp.concatenate(
        [first * cosine - second * sine, second * cosine + first * sine], axis=-1
    )


def doc_info(lengths, index):
    ends = jnp.cumsum(lengths)
    starts = ends - lengths
    segment = jnp.sum((index[:, None] >= ends[None, :-1]).astype(jnp.int32), axis=1)
    hit = segment[:, None] == jnp.arange(lengths.shape[0], dtype=jnp.int32)[None, :]
    first = jnp.sum(jnp.where(hit, starts[None, :], 0), axis=1)
    segment = jnp.where(index < 0, -1, segment)
    return (segment, index - first)


def dot(a, b, dims=(((1,), (0,)), ((), ()))):
    return lax.dot_general(a, b, dims, preferred_element_type=F32)


GELU_SCALE = math.sqrt(2.0 / math.pi)
GELU_CUBE = 0.044715


def join(pieces, whole):
    at = 0
    for piece in pieces:
        whole[at : at + piece.shape[0], :] = piece[...]
        at += piece.shape[0]


def feed_kernel(count, *refs):
    pieces, weights, (x, *saved, out) = (refs[:count], refs[count : count + 6], refs[count + 6 :])
    join(pieces, x)

    @pl.loop(0, x.shape[0] // TILE)
    def _(step):
        lines = pl.ds(pl.multiple_of(step * TILE, TILE), TILE)
        block = x[lines, :]
        total = None
        for half in range(2):
            gate_w, up_w, down_w = weights[half::2]
            gate_s, up_s, hidden_s = saved[half::2]
            gate = dot(block, gate_w[...], CONTRACT_LAST)
            upward = dot(block, up_w[...], CONTRACT_LAST)
            bend = jnp.tanh(GELU_SCALE * (gate + GELU_CUBE * gate * gate * gate))
            hidden = (0.5 * gate * (1.0 + bend) * upward).astype(LOW)
            gate_s[lines, :] = gate.astype(LOW)
            up_s[lines, :] = upward.astype(LOW)
            hidden_s[lines, :] = hidden
            part = dot(hidden, down_w[...])
            total = part if total is None else total + part
        out[lines, :] = total.astype(LOW)


def back_kernel(count, *refs):
    pieces, weights = (refs[:count], refs[count : count + 6])
    gates, ups = (refs[count + 6 : count + 8], refs[count + 8 : count + 10])
    grad, *saved, out = refs[count + 10 :]
    join(pieces, grad)

    @pl.loop(0, grad.shape[0] // TILE)
    def _(step):
        lines = pl.ds(pl.multiple_of(step * TILE, TILE), TILE)
        block = grad[lines, :]
        total = None
        for half in range(2):
            gate_w, up_w, down_w = weights[half::2]
            grad_hidden = dot(block, down_w[...], CONTRACT_LAST)
            gate = gates[half][lines, :].astype(F32)
            upward = ups[half][lines, :].astype(F32)
            square = gate * gate
            bend = jnp.tanh(GELU_SCALE * gate * (1.0 + GELU_CUBE * square))
            rise = 0.5 * (1.0 + bend)
            slope = rise + 0.5 * gate * (1.0 - bend * bend) * (
                GELU_SCALE * (1.0 + 3.0 * GELU_CUBE * square)
            )
            grad_gate = (grad_hidden * upward * slope).astype(LOW)
            grad_up = (grad_hidden * gate * rise).astype(LOW)
            saved[half][lines, :] = grad_gate
            saved[2 + half][lines, :] = grad_up
            part = dot(grad_gate, gate_w[...]) + dot(grad_up, up_w[...])
            total = part if total is None else total + part
        out[lines, :] = total.astype(LOW)


def rows_kernel(count, *refs):
    out = refs[-1]
    hidden, width = (refs[0].shape[1], refs[2].shape[1])
    for k in range(count):
        left, right = (refs[4 * k : 4 * k + 2], refs[4 * k + 2 : 4 * k + 4])
        columns = slice(k * width, (k + 1) * width)
        total = dot(left[0][...], right[0][...], CONTRACT_FIRST)
        total = total + dot(left[1][...], right[1][...], CONTRACT_FIRST)
        if len(refs) > 4 * count + 1:
            total = total + refs[4 * count][:hidden, columns].astype(F32)
        out[:hidden, columns] = total.astype(LOW)
    out[hidden:, :] = jnp.zeros((out.shape[0] - hidden, out.shape[1]), LOW)


def head_slices(queries, head_size):
    return [slice(at, at + head_size) for at in range(0, queries.shape[1], head_size)]


def masked_softmax(query, keys, mask):
    scores = jnp.where(mask > 0, dot(query, keys, CONTRACT_LAST), MASKED)
    expo = jnp.exp(scores - jnp.max(scores, axis=-1, keepdims=True))
    return expo / jnp.sum(expo, axis=-1, keepdims=True)


def attend_kernel(query, both, mask, weight, inputs, gains, mixed, projected, residual, normed):
    size = both.shape[1] // 2
    keys, values, allowed = (both[:, :size], both[:, size:], mask[...])
    for columns in head_slices(query, size):
        probs = masked_softmax(query[:, columns], keys, allowed)
        mixed[:, columns] = dot(probs.astype(LOW), values).astype(LOW)
    lines = dot(mixed[...], weight[...])
    projected[...] = lines
    lines = inputs[...].astype(F32) + norm_rows(lines, gains[0:1, :])
    residual[...] = lines
    normed[...] = norm_rows(lines, gains[1:2, :]).astype(LOW)


def attend_back_kernel(
    grad, weight, query, both, mask, linear, turns, gain, out, grad_gain, own, away, total
):
    size = both.shape[1] // 2
    half = size // 2
    keys, values, allowed = (both[:, :size], both[:, size:], mask[...])
    cosine, sine = (turns[:, :half], turns[:, half:])
    grad_gain[...] = jnp.zeros_like(grad_gain)
    for head, columns in enumerate(head_slices(query, size)):
        probs = masked_softmax(query[:, columns], keys, allowed)
        grad_mixed = dot(grad[...], weight[columns, :], CONTRACT_LAST).astype(LOW)
        grad_probs = dot(grad_mixed, values, CONTRACT_LAST)
        inner = jnp.sum(grad_probs * probs, axis=-1, keepdims=True)
        grad_scores = (probs * (grad_probs - inner)).astype(LOW)
        grad_keys = dot(grad_scores, query[:, columns], CONTRACT_FIRST)
        grad_values = dot(probs.astype(LOW), grad_mixed, CONTRACT_FIRST)
        if head == 0:
            total[:, :size] = grad_keys
            total[:, size:] = grad_values
        else:
            total[:, :size] += grad_keys
            total[:, size:] += grad_values
        turned_grad = dot(grad_scores, keys).astype(LOW).astype(F32) * size**-0.5
        first, second = (turned_grad[:, :half], turned_grad[:, half:])
        grad_normed = jnp.concatenate(
            [first * cosine + second * sine, second * cosine - first * sine], axis=1
        )
        lines = linear[:, columns]
        scale = lax.rsqrt(jnp.mean(lines * lines, axis=-1, keepdims=True) + EPSILON)
        grad_gain[0:1, :] += jnp.sum(grad_normed * lines * scale, axis=0, keepdims=True)
        grad_normed = grad_normed * gain[0:1, :]
        share = jnp.mean(grad_normed * lines, axis=-1, keepdims=True)
        out[:, columns] = (scale * grad_normed - lines * (scale * scale * scale * share)).astype(LOW)
    kept = own.shape[0]
    own[...] = total[:kept, :]
    away[...] = total[kept:, :].astype(LOW)


def wide_kernel(inputs, query, mixed, grad, mine, away, block):
    devices, columns = (mine.shape[0] * 2 // block.shape[0], query.shape[1])
    query_grad = dot(inputs[...], query[...])
    output_grad = dot(mixed[...], grad[...])
    own, lines = (query_grad.shape[0] // devices, output_grad.shape[0] // devices)
    rest = output_grad.shape[1] - columns
    size = lines * rest // columns
    for number in range(devices):
        part = output_grad[number * lines : (number + 1) * lines]
        block[:own, :] = query_grad[number * own : (number + 1) * own]
        block[own : own + lines, :] = part[:, :columns]
        for k in range(columns // rest):
            block[own + lines :, k * rest : (k + 1) * rest] = part[
                k * size : (k + 1) * size, columns:
            ]
        out = away if number % 2 else mine
        at = number // 2 * block.shape[0]
        out[at : at + block.shape[0], :] = block[...].astype(LOW)


def pair_kernel(inputs, pair, gains, mine, away, block):
    pair_grad = dot(inputs[...], pair[...])
    devices = mine.shape[0] * 2 // block.shape[0]
    own = pair_grad.shape[0] // devices
    more = block.shape[0] - own
    for number in range(devices):
        block[:own, :] = pair_grad[number * own : (number + 1) * own]
        block[own:, :] = gains[number * more : (number + 1) * more, :]
        out = away if number % 2 else mine
        at = number // 2 * block.shape[0]
        out[at : at + block.shape[0], :] = block[...].astype(LOW)


def block_call(kernel, lines, columns, args):
    half = jax.ShapeDtypeStruct((NZ * NH * lines, columns), LOW)
    flops = 4 * args[0].shape[0] * args[0].shape[1] * columns
    return whole_call(kernel, [half, half], flops, args, [pltpu.VMEM((lines, columns), F32)])


def whole_call(kernel, shapes, flops, args, scratch=()):
    moved = sum(math.prod(a.shape) * 2 for a in (*args, *shapes))
    return pl.pallas_call(
        kernel,
        out_shape=shapes,
        in_specs=[pl.BlockSpec(memory_space=pltpu.VMEM)] * len(args),
        out_specs=[pl.BlockSpec(memory_space=pltpu.VMEM)] * len(shapes),
        scratch_shapes=scratch,
        compiler_params=pltpu.CompilerParams(vmem_limit_bytes=VMEM),
        cost_estimate=pl.CostEstimate(flops=flops, bytes_accessed=moved, transcendentals=0),
    )(*args)


def feed(pieces, weights):
    rows, (hidden, width) = (sum(p.shape[0] for p in pieces), weights[0].shape)
    shapes = [jax.ShapeDtypeStruct((rows, n), LOW) for n in [width] + [hidden] * 6 + [width]]
    return whole_call(
        functools.partial(feed_kernel, len(pieces)),
        shapes,
        12 * rows * hidden * width,
        (*pieces, *weights),
    )


def feed_back(pieces, weights, gates, ups):
    rows, (hidden, width) = (sum(p.shape[0] for p in pieces), weights[0].shape)
    shapes = [jax.ShapeDtypeStruct((rows, n), LOW) for n in [width] + [hidden] * 4 + [width]]
    return whole_call(
        functools.partial(back_kernel, len(pieces)),
        shapes,
        12 * rows * hidden * width,
        (*pieces, *weights, *gates, *ups),
    )


def row_gradients(pairs, added=()):
    args = [a for left, right in pairs for a in (*left, *right)]
    rows, hidden = args[0].shape
    width = args[2].shape[1]
    lines = hidden + -hidden % ROW_GRANULE
    return whole_call(
        functools.partial(rows_kernel, len(pairs)),
        [jax.ShapeDtypeStruct((lines, len(pairs) * width), LOW)],
        4 * len(pairs) * rows * hidden * width,
        (*args, *added),
    )[0]


def local(
    tokens,
    lengths,
    cotangent,
    pre_attention,
    post_attention,
    pre_forward,
    post_forward,
    query_gain,
    key_gain,
    query_weight,
    key_weight,
    value_weight,
    output_weight,
    gate_rows,
    up_rows,
    down_rows,
):
    rows = tokens.shape[0]
    width = tokens.shape[1]
    head_size = key_weight.shape[1]
    heads = query_weight.shape[1] // head_size
    features = heads * head_size
    span = features + 2 * head_size
    devices = NZ * NH * NC
    own_rows = query_weight.shape[0]
    own_gain = query_gain.shape[0]
    chips_back = (WINDOW + NC * rows - 1) // (NC * rows)
    shard = lax.axis_index("fsdp")
    local_index = shard * rows + jnp.arange(rows, dtype=jnp.int32)
    other = shard + 1 - 2 * (shard % NC)
    key_index = jnp.concatenate(
        [
            (core - back * NC) * rows + jnp.arange(rows, dtype=jnp.int32)
            for core in (shard, other)
            for back in range(chips_back, -1, -1)
        ]
    )
    query_seg, query_pos = doc_info(lengths[0], local_index)
    key_seg, key_place = doc_info(lengths[0], key_index)
    distance = local_index[:, None] - key_index[None, :]
    allowed = (query_seg[:, None] == key_seg[None, :]) & (distance >= 0) & (distance < WINDOW)

    gains = (pre_attention, post_attention, pre_forward, post_forward, query_gain, key_gain)
    lines = [jnp.pad(g[None, :], ((0, 0), (0, span - g.shape[0]))) for g in gains]
    packed = jnp.concatenate(
        [
            jnp.concatenate([query_weight, key_weight, value_weight], axis=1),
            *lines,
            jnp.zeros((GAIN_LINES - len(lines), span), LOW),
        ],
        axis=0,
    )
    weight_out = lax.all_gather(output_weight, "fsdp", axis=0, tiled=True)
    feed_own = (gate_rows, up_rows, down_rows)
    first_all, feed_own = in_offset_order(gather_chips(packed), feed_own)
    feed_other = tuple(swap(w) for w in feed_own)
    weight_in = first_all[:, :own_rows].reshape(width, span)
    gain_all = to_mesh_order(first_all[:, own_rows:, :own_rows]).astype(F32)
    gain_pre_att, gain_post_att, gain_pre_fwd, gain_post_fwd = (
        gain_all[:, k].reshape(width) for k in range(4)
    )
    gain_query, gain_key = (gain_all[:, 4 + k, :own_gain].reshape(head_size) for k in range(2))

    inputs = tokens.astype(F32)
    normed_one, pull_one = jax.vjp(norm_rows, inputs, gain_pre_att)
    normed_low = normed_one.astype(LOW)
    normed_rel = to_relative(normed_low.T.reshape(devices, own_rows, rows)).reshape(width, rows)
    linear = dot(normed_rel, weight_in, CONTRACT_FIRST)
    query_lin = linear[:, :features]
    key_lin = linear[:, features : features + head_size]
    value_low = linear[:, features + head_size :].astype(LOW)

    table = rope_table(query_pos, head_size)
    query_heads = norm_rows(query_lin.reshape(rows, heads, head_size), gain_query)
    query_value = (rotate(query_heads, table) * head_size**-0.5).reshape(rows, features)

    def key_side(lin, gain):
        return rotate(norm_rows(lin[:, None, :], gain), table)[:, 0, :]

    key_value, pull_key = jax.vjp(key_side, key_lin, gain_key)
    query_low = query_value.astype(LOW)
    key_low = key_value.astype(LOW)
    outgoing = jnp.concatenate([key_low, value_low], axis=1)
    outgoing, feed_other = lax.optimization_barrier((outgoing, feed_other))
    feed_weights = [w for both in zip(feed_own, feed_other) for w in both]
    arrived = [shifted(outgoing, "fsdp", NC * back) for back in range(chips_back, 0, -1)]
    mine = jnp.concatenate(arrived + [outgoing], axis=0)
    both = jnp.concatenate([mine, swap(mine)], axis=0)
    mask = allowed.astype(F32)
    gain_lines = jnp.stack([gain_post_att, gain_pre_fwd])
    line, wide = ((rows, width), (rows, features))
    mixed_low, projected, residual_one, normed_two_low = whole_call(
        attend_kernel,
        [
            jax.ShapeDtypeStruct(wide, LOW),
            jax.ShapeDtypeStruct(line, F32),
            jax.ShapeDtypeStruct(line, F32),
            jax.ShapeDtypeStruct(line, LOW),
        ],
        2 * rows * features * (width + 2 * both.shape[0]),
        (query_low, both, mask, weight_out, tokens, gain_lines),
    )
    mixed_rel = to_relative(mixed_low.T.reshape(devices, -1, rows)).reshape(features, rows)
    _, pull_two = jax.vjp(norm_rows, projected, gain_post_att)
    _, pull_three = jax.vjp(norm_rows, residual_one, gain_pre_fwd)

    normed_of = gather_chips(normed_two_low)
    acts, sent = ([], [])
    for offsets in (NEAR, FAR):
        pieces = [piece for p in offsets for piece in normed_of[p]]
        *kept, down = feed(pieces, feed_weights)
        acts.append(kept)
        sent.append(handed(offsets, down))
    turns, gain_query_line = (jnp.concatenate(table, axis=1), gain_query[None, :])
    sent[1][-1], mixed_rel, turns, gain_query_line = lax.optimization_barrier(
        (sent[1][-1], mixed_rel, turns, gain_query_line)
    )
    down_sum = sum_of(sent)
    fed, pull_four = jax.vjp(norm_rows, down_sum, gain_post_fwd)
    output = (residual_one + fed).astype(LOW)
    grad_out = cotangent.astype(F32)
    grad_down, grad_post_fwd = pull_four(grad_out)
    grad_down_of = gather_chips(grad_down.astype(LOW))
    backs, sent = ([], [])
    for offsets, kept in zip((NEAR, FAR), acts):
        pieces = [piece for p in offsets for piece in grad_down_of[p]]
        *grads, back = feed_back(pieces, feed_weights, kept[1:3], kept[3:5])
        backs.append(grads)
        sent.append(handed(offsets, back))
    backs, sent[0] = lax.optimization_barrier((backs, sent[0]))
    normed_chunks, grad_chunks = ([kept[0] for kept in acts], [grads[0] for grads in backs])
    products = [
        [
            ([grads[1 + core] for grads in backs], normed_chunks),
            ([grads[3 + core] for grads in backs], normed_chunks),
            ([kept[5 + core] for kept in acts], grad_chunks),
        ]
        for core in range(NC)
    ]
    hidden_rows = gate_rows.shape[0]
    rows_sum = row_gradients(products[0]).astype(F32)
    rows_sum = (rows_sum + swap(row_gradients(products[1])).astype(F32)).astype(LOW)
    sent[1][-1], rows_sum = lax.optimization_barrier((sent[1][-1], rows_sum))
    grad_normed_two = sum_of(sent)
    rows_share = y_part(rows_sum)

    extra_three, grad_pre_fwd = pull_three(grad_normed_two)
    grad_residual = grad_out + extra_three
    grad_projected, grad_post_att = pull_two(grad_residual)
    grad_proj_low = grad_projected.astype(LOW)
    half = (chips_back + 1) * rows
    query_lin_low, grad_query_gain, grad_own, grad_away = whole_call(
        attend_back_kernel,
        [
            jax.ShapeDtypeStruct(wide, LOW),
            jax.ShapeDtypeStruct((1, head_size), F32),
            jax.ShapeDtypeStruct((half, 2 * head_size), F32),
            jax.ShapeDtypeStruct((half, 2 * head_size), LOW),
        ],
        2 * rows * features * (width + 5 * both.shape[0]),
        (
            grad_proj_low,
            weight_out,
            query_low,
            both,
            mask,
            query_lin,
            turns,
            gain_query_line,
        ),
        [pltpu.VMEM((2 * half, 2 * head_size), F32)],
    )
    grad_query_gain = grad_query_gain[0]
    grad_both = grad_own + swap(grad_away).astype(F32)
    grad_both, query_lin_low, grad_proj_low = lax.optimization_barrier(
        (grad_both, query_lin_low, grad_proj_low)
    )
    lines = own_rows + (features // devices) * width // features
    sums = chip_sums(
        *block_call(
            wide_kernel, lines, features, (normed_rel, query_lin_low, mixed_rel, grad_proj_low)
        )
    )
    owned_both = grad_both[chips_back * rows :]
    for back in range(1, chips_back + 1):
        piece = grad_both[(chips_back - back) * rows : (chips_back - back + 1) * rows]
        owned_both = owned_both + shifted(piece.astype(LOW), "fsdp", -NC * back).astype(F32)
    owned_both, sums = lax.optimization_barrier((owned_both, sums))
    rows_share, _ = lax.optimization_barrier((rows_share, sums))
    wide_part = z_sums(sums)
    rows_share = x_sum(rows_share)
    grad_key_low = owned_both[:, :head_size].astype(LOW)
    grad_value_low = owned_both[:, head_size:].astype(LOW)
    grad_key_lin, grad_key_gain = pull_key(grad_key_low.astype(F32))
    pair_low = jnp.concatenate([grad_key_lin.astype(LOW), grad_value_low], axis=1)
    grad_linear = jnp.concatenate([query_lin_low, pair_low], axis=1)
    grad_normed_rel = dot(weight_in, grad_linear, CONTRACT_LAST)
    grad_normed_one = to_mesh_order(grad_normed_rel.reshape(devices, own_rows, rows))
    grad_normed_one = grad_normed_one.reshape(width, rows).T
    extra_one, grad_pre_att = pull_one(grad_normed_one)
    grad_inputs = grad_residual + extra_one
    gain_grads = jnp.stack(
        [
            jnp.pad(g.reshape(devices, -1), ((0, 0), (0, own_rows - g.shape[0] // devices)))
            for g in (
                grad_pre_att,
                grad_post_att,
                grad_pre_fwd,
                grad_post_fwd,
                grad_query_gain,
                grad_key_gain,
            )
        ],
        axis=1,
    )
    gain_grads = to_relative(gain_grads)
    gain_grads = jnp.pad(
        gain_grads,
        ((0, 0), (0, GAIN_LINES - gain_grads.shape[1]), (0, 2 * head_size - own_rows)),
    ).reshape(-1, 2 * head_size)
    pair_sums = chip_sums(
        *block_call(
            pair_kernel, own_rows + GAIN_LINES, 2 * head_size, (normed_rel, pair_low, gain_grads)
        )
    )
    pair_sums, wide_part, rows_share = lax.optimization_barrier(
        (pair_sums, wide_part, rows_share)
    )
    rows_near = y_near(rows_share)
    wide_part = pair_sum(wide_part)
    pair_part = pair_sum(z_sums(pair_sums))
    pair_part, rows_near = lax.optimization_barrier((pair_part, rows_near))
    rows_whole = y_whole(rows_share, *rows_near)
    middle = pair_part.shape[0] // 2
    share = jnp.concatenate(
        [wide_part, jnp.concatenate([pair_part[:middle], pair_part[middle:]], axis=1)], axis=0
    )
    spare = -share.shape[0] % (16 * NY)
    share = jnp.pad(share, ((0, spare), (0, 0))).astype(LOW)
    share, rows_whole = rep_sum(share, rows_whole)
    owned_query = share[:own_rows]
    owned_output = unfolded(share[own_rows : wide_part.shape[0]], width)
    pair_lines = share[wide_part.shape[0] : wide_part.shape[0] + middle]
    owned_pair = jnp.concatenate(jnp.split(pair_lines, 2, axis=1), axis=0)
    owned_gains = [owned_pair[own_rows + k, :own_rows] for k in range(4)]
    owned_gains += [owned_pair[own_rows + 4 + k, :own_gain] for k in range(2)]
    owned_pair = owned_pair[:own_rows]
    rows_whole = rows_whole[:hidden_rows].astype(F32)
    return (
        output,
        grad_inputs,
        *owned_gains,
        owned_query,
        owned_pair[:, :head_size],
        owned_pair[:, head_size:],
        owned_output,
        rows_whole[:, :width],
        rows_whole[:, width : 2 * width],
        rows_whole[:, 2 * width :],
    )


def solution(mesh):
    tokens, weight, vector = (P(("rep", "fsdp"), None), P("fsdp", None), P("fsdp"))
    return jax.shard_map(
        local,
        mesh=mesh,
        in_specs=(tokens, P("rep", None), tokens) + (vector,) * 6 + (weight,) * 7,
        out_specs=(tokens, tokens) + (vector,) * 6 + (weight,) * 7,
        check_vma=False,
    )
```
